512 devices in a mesh: section: 4 (over x), expert: 32 (over y_lo, z, core), dp: 4 (over y_hi).
Axes of the slice: x: 4, y: 8 (y_hi: 4, y_lo: 2; y = y_hi * 2 + y_lo), z: 8, core: 2. Of those that a mesh axis runs over, the one named last changes fastest.
Arguments:
- stream_in: bfloat16 [2, 2, 4096, 3584], P(None, None, ('expert', 'dp'), 'section'), may hold values from -6 to 6
- cotangent: bfloat16 [2, 2, 4096, 3584], P(None, None, ('expert', 'dp'), 'section'), may hold values from -6 to 6
- route_ids: int32 [2, 2, 2, 4096, 2], P(None, None, None, ('expert', 'dp')), may hold values from 0 to 31, all different within a row; in each aligned block of 32 rows (0 to 31, 32 to 63, ..., all dimensions but the last counted through in order) at most 4 rows name the same one
- route_gates: float32 [2, 2, 2, 4096, 2], P(None, None, None, ('expert', 'dp')), may hold values from 0.1 to 1
- norm_gain: float32 [2, 3584], replicated, may hold values from 0.25 to 1.75
- up_weight: bfloat16 [4, 32, 3584, 512], P('section', 'expert', 'dp'), may hold values from -0.09375 to 0.09375
- down_weight: bfloat16 [4, 32, 512, 3584], P('section', 'expert', None, 'dp'), may hold values from -0.1875 to 0.1875
Outputs:
- grad_up: bfloat16 [4, 32, 3584, 512], P('section', 'expert', 'dp')
- grad_down: bfloat16 [4, 32, 512, 3584], P('section', 'expert', None, 'dp')
The draws below stay inside these ranges and needn't reach their ends.
Inputs may be any that keep to these rules, and one draw needn't show every extreme that they name: `route_ids`: each token names 2 different experts in each layer; among the tokens of one micro-batch of one device in one layer (aligned blocks of 32 rows) no expert is named more than 4 times, and some block names an expert exactly 4 times.
All inputs are finite; a program needn't handle non-finite values.
Results may differ from the reference program's by a relative error of at most 0.025.
Values may be sent and summed in bfloat16 or wider, within the bound.
A program may use at most 128 MiB of HBM per device.

```python
import math
import jax
import jax.numpy as jnp
import numpy as np
from jax import lax

D = 3584
EH = 1024
TOP = 2
MICRO = 2
TOKMB = 32
LAYERS = 2
EXPERTS = 32
CAP = 4
TOKENS = 4096
N_DP = 4


def steps_of(stream_key, shape, cuts, low, largest):
    factor_of, own = 1.0, jax.random.fold_in(stream_key, 6)
    for dim, parts in cuts:
        steps = jnp.exp(jax.random.uniform(jax.random.fold_in(own, dim), (parts,), jnp.float32, low / len(cuts), largest / len(cuts)))
        factor_of = factor_of * jnp.repeat(steps, shape[dim] // parts).reshape([-1 if axis == dim else 1 for axis in range(len(shape))])
    return factor_of


def assign_block(stream_key, own, number, rows, amount, top, reach, skew):
    order = jax.random.permutation(stream_key, amount)
    heavy_load, usual = portions_of(amount, rows * top, reach, skew, True), portions_of(amount, rows * top, reach, skew, False)
    places = jnp.arange(amount)

    def named(sizes, offset_by):
        used = int((sizes > 0).sum())
        fixed = max(1, used // 4)
        shifted = fixed + (places - fixed + offset_by * (used - fixed)) % max(1, amount - fixed)
        return jnp.zeros((amount,), jnp.int32).at[order[jnp.where(places < fixed, places, shifted)]].set(jnp.asarray(sizes, jnp.int32))

    sizes = jnp.where(number % 4 == 0, named(heavy_load, number // 4), named(usual, number - number // 4 - 1))
    mixed = jax.random.permutation(jax.random.fold_in(own, 3), amount)
    giver, taker = mixed[0:amount // 2 * 2:2], mixed[1:amount // 2 * 2:2]
    room = jnp.minimum(sizes[giver] - 1, reach - sizes[taker]) // 2
    room = jnp.where((giver == order[0]) | (taker == order[0]) | (sizes[taker] == 0), 0, jnp.maximum(room, 0))
    shifted = jax.random.randint(jax.random.fold_in(own, 4), (amount // 2,), 0, 1 << 20) % (room + 1)
    sizes = sizes.at[giver].add(-shifted).at[taker].add(shifted)
    items = jnp.searchsorted(jnp.cumsum(sizes), jnp.arange(rows * top), side="right").astype(jnp.int32)
    listing = items.reshape(top, rows).T
    listing = listing[jax.random.permutation(jax.random.fold_in(own, 1), rows)]
    offset_by = jax.random.randint(jax.random.fold_in(own, 2), (rows, 1), 0, top)
    return jnp.take_along_axis(listing, (jnp.arange(top)[None, :] + offset_by) % top, axis=1)


def portions_of(number_of, total, bound, lean, full):
    loads = [(1 << 20) // math.isqrt(grade ** lean) + 1 for grade in range(1, number_of + 1)]
    largest = bound if full else min(bound, max(-(-total // number_of), total * loads[0] // sum(loads)))
    least = 1 if total - largest >= number_of - 1 else 0
    given, spare = [largest] + [least] * (number_of - 1), total - largest - least * (number_of - 1)
    while spare > 0:
        movable = [i for i in range(1, number_of) if given[i] < largest] or [i for i in range(1, number_of) if given[i] < bound]
        mass, left = sum([loads[i] for i in movable]), spare
        for i in movable:
            extra = min(bound - given[i], max(1, left * loads[i] // mass), spare)
            given[i] = given[i] + extra
            spare = spare - extra
    return np.array(given)


def centred(rng, shape, spread, limit, split=(), held_as=jnp.bfloat16):
    loudness = steps_of(rng, shape, split, -0.22, 0.18) if split else 1.0
    result = jax.random.normal(rng, shape, jnp.float32) * spread * loudness
    return jnp.minimum(jnp.maximum(result, -limit), limit).astype(held_as)


def setup_inputs(seed: int = 0) -> dict:
    key_of = jax.random.split(jax.random.key(seed), 8)
    stream_in = centred(key_of[0], (2, MICRO, TOKENS, D), 1.0, 6.0, ((2, 128), (3, 4)))
    cotangent = centred(key_of[1], (2, MICRO, TOKENS, D), 1.0, 6.0, ((2, 128), (3, 4)))
    route_ids_keys = jax.random.split(jax.random.fold_in(key_of[2], 1), LAYERS * 2 * MICRO * TOKENS // TOKMB)
    route_ids_turns = jax.random.permutation(jax.random.fold_in(key_of[2], 3), LAYERS * 2 * MICRO * TOKENS // TOKMB)
    route_ids = jax.vmap(lambda own, number: assign_block(jax.random.fold_in(key_of[2], 2), own, number, TOKMB, EXPERTS, TOP, CAP, 2))(route_ids_keys, route_ids_turns).reshape((LAYERS, 2, MICRO, TOKENS, TOP))
    route_gates = jnp.clip(0.1 + 0.9 * jax.random.uniform(key_of[3], (LAYERS, 2, MICRO, TOKENS, TOP), jnp.float32) ** steps_of(key_of[3], (LAYERS, 2, MICRO, TOKENS, TOP), ((3, 128),), -0.2, 0.2), 0.1, 1.0)
    norm_gain = jnp.clip(1.0 + 0.15 * jax.random.normal(key_of[4], (LAYERS, D), jnp.float32), 0.25, 1.75)
    up_weight = centred(key_of[5], (2 * LAYERS, EXPERTS, D, EH // 2), D ** -0.5, 0.09375, ((0, 4), (1, 32), (2, 4)))
    down_weight = centred(key_of[6], (2 * LAYERS, EXPERTS, EH // 2, D), EH ** -0.5, 0.1875, ((0, 4), (1, 32), (3, 4)))
    return dict(stream_in=stream_in, cotangent=cotangent, route_ids=route_ids, route_gates=route_gates, norm_gain=norm_gain, up_weight=up_weight, down_weight=down_weight)


EPSILON = 1e-06

def slot_position(chosen):
    block_count = chosen.shape[0] // TOKMB
    blocks = chosen.reshape(block_count, TOKMB * TOP)
    matches = (blocks[:, :, None] == jnp.arange(EXPERTS, dtype=jnp.int32)[None, None, :]).astype(jnp.int32)
    earlier = jnp.cumsum(matches, axis=1) - matches
    return lax.optimization_barrier(jnp.sum(earlier * matches, axis=2)).reshape(chosen.shape[0], TOP).astype(jnp.int32)

def block_of(chosen):
    rows_here = jnp.arange(chosen.shape[0], dtype=jnp.int32) // TOKMB
    return jnp.broadcast_to(rows_here[:, None], chosen.shape).astype(jnp.int32)

def normalize(layer_in, gain_row):
    as_float = layer_in.astype(jnp.float32)
    scale_inv = lax.rsqrt(lax.optimization_barrier(jnp.mean(as_float * as_float, axis=-1, keepdims=True)) + EPSILON)
    return (as_float, scale_inv, (as_float * scale_inv * gain_row).astype(jnp.bfloat16))

def to_table(assigned, chosen, block_ids, position):
    block_count = chosen.shape[0] // TOKMB
    table = jnp.zeros((EXPERTS, block_count, CAP, D), jnp.bfloat16)
    table = table.at[chosen, block_ids, position].set(assigned)
    return table.reshape(EXPERTS, block_count * CAP, D)

def from_table(table, chosen, block_ids, position):
    block_count = chosen.shape[0] // TOKMB
    return table.reshape(EXPERTS, block_count, CAP, D)[chosen, block_ids, position]

def rounded_sum(partials):
    kept = lax.optimization_barrier(partials.astype(jnp.bfloat16))
    return lax.optimization_barrier(jnp.sum(kept.astype(jnp.float32), axis=0))

def hidden_pre(rows, up_e):
    rows_f = rows.astype(jnp.float32).reshape(rows.shape[0], N_DP, D // N_DP)
    up_f = up_e.astype(jnp.float32).reshape(2, N_DP, D // N_DP, EH // 2)
    return rounded_sum(jnp.einsum('rgq,hgqk->ghrk', rows_f, up_f))

def expert_rows(act, down_e):
    return rounded_sum(jnp.einsum('hrk,hkd->hrd', act.astype(jnp.float32), down_e.astype(jnp.float32))).astype(jnp.bfloat16)

def hidden_grad(grads, down_e, pre_act):
    grads_f = grads.astype(jnp.float32).reshape(grads.shape[0], N_DP, D // N_DP)
    down_f = down_e.astype(jnp.float32).reshape(2, EH // 2, N_DP, D // N_DP)
    act_grad = rounded_sum(jnp.einsum('rgq,hkgq->ghrk', grads_f, down_f))
    sigmoid_val = jax.nn.sigmoid(pre_act)
    return (act_grad * sigmoid_val * (1.0 + pre_act * (1.0 - sigmoid_val))).astype(jnp.bfloat16)

def row_grad(pre_grad, up_e):
    return rounded_sum(jnp.einsum('hrk,hdk->hrd', pre_grad.astype(jnp.float32), up_e.astype(jnp.float32))).astype(jnp.bfloat16)

def route_setup(layer_in, gain_row, chosen, gate_raw):
    as_float, scale_inv, normed = normalize(layer_in, gain_row)
    block_ids = block_of(chosen)
    position = slot_position(chosen)
    shares = gate_raw / lax.optimization_barrier(jnp.sum(gate_raw, axis=-1, keepdims=True))
    assigned = jnp.broadcast_to(normed[:, None, :], (normed.shape[0], TOP, D))
    rows_table = to_table(assigned, chosen, block_ids, position)
    return (as_float, scale_inv, block_ids, position, shares, rows_table)

def layer_forward(layer_in, gain_row, chosen, gate_raw, up_l, down_l):
    as_float, scale_inv, block_ids, position, shares, rows_table = route_setup(layer_in, gain_row, chosen, gate_raw)

    def one_expert(items):
        rows, up_e, down_e = items
        act = jax.nn.silu(hidden_pre(rows, up_e)).astype(jnp.bfloat16)
        return expert_rows(act, down_e)
    out_table = lax.map(one_expert, (rows_table, up_l, down_l))
    picked = from_table(out_table, chosen, block_ids, position).astype(jnp.float32)
    return (as_float + lax.optimization_barrier(jnp.sum(shares[:, :, None] * picked, axis=1))).astype(jnp.bfloat16)

def layer_backward(layer_in, incoming, gain_row, chosen, gate_raw, up_l, down_l):
    as_float, scale_inv, block_ids, position, shares, rows_table = route_setup(layer_in, gain_row, chosen, gate_raw)
    incoming_f = incoming.astype(jnp.float32)
    out_grad = (shares[:, :, None] * incoming_f[:, None, :]).astype(jnp.bfloat16)
    grad_table = to_table(out_grad, chosen, block_ids, position)

    def one_expert(items):
        rows, grads, up_e, down_e = items
        pre_act = hidden_pre(rows, up_e)
        act = jax.nn.silu(pre_act).astype(jnp.bfloat16)
        pre_grad = hidden_grad(grads, down_e, pre_act)
        back = row_grad(pre_grad, up_e)
        part_up = jnp.einsum('rd,hrk->hdk', rows.astype(jnp.float32), pre_grad.astype(jnp.float32))
        part_down = jnp.einsum('hrk,rd->hkd', act.astype(jnp.float32), grads.astype(jnp.float32))
        return (back, part_up, part_down)
    in_table, part_up, part_down = lax.map(one_expert, (rows_table, grad_table, up_l, down_l))
    normed_grad = lax.optimization_barrier(jnp.sum(from_table(in_table, chosen, block_ids, position).astype(jnp.float32), axis=1))
    scaled = normed_grad * gain_row
    layer_grad = incoming_f + scale_inv * scaled - as_float * scale_inv ** 3 * lax.optimization_barrier(jnp.mean(as_float * scaled, axis=-1, keepdims=True))
    return (layer_grad.astype(jnp.bfloat16), part_up, part_down)

def layer_weights(weight, layer_pos):
    return jnp.moveaxis(weight[2 * layer_pos:2 * layer_pos + 2], 0, 1)

def reference(stream_in, cotangent, route_ids, route_gates, norm_gain, up_weight, down_weight):
    gain_rows = norm_gain.astype(jnp.float32)
    ups = [layer_weights(up_weight, layer_pos) for layer_pos in range(LAYERS)]
    downs = [layer_weights(down_weight, layer_pos) for layer_pos in range(LAYERS)]
    acc_up = [jnp.zeros((EXPERTS, 2, D, EH // 2), jnp.float32) for layer_pos in range(LAYERS)]
    acc_down = [jnp.zeros((EXPERTS, 2, EH // 2, D), jnp.float32) for layer_pos in range(LAYERS)]
    for direction in range(2):
        if direction == 0:
            layer_order = list(range(LAYERS))
        else:
            layer_order = list(range(LAYERS - 1, -1, -1))
        for batch_pos in range(MICRO):
            current = stream_in[direction, batch_pos]
            saved_inputs = []
            for layer_pos in layer_order:
                saved_inputs.append(current)
                current = layer_forward(current, gain_rows[layer_pos], route_ids[layer_pos, direction, batch_pos], route_gates[layer_pos, direction, batch_pos], ups[layer_pos], downs[layer_pos])
            incoming = cotangent[direction, batch_pos]
            for layer_pos, layer_in in zip(reversed(layer_order), reversed(saved_inputs)):
                incoming, part_up, part_down = layer_backward(layer_in, incoming, gain_rows[layer_pos], route_ids[layer_pos, direction, batch_pos], route_gates[layer_pos, direction, batch_pos], ups[layer_pos], downs[layer_pos])
                acc_up[layer_pos] = acc_up[layer_pos] + part_up
                acc_down[layer_pos] = acc_down[layer_pos] + part_down
    grad_up = jnp.concatenate([jnp.moveaxis(total, 1, 0) for total in acc_up], axis=0).astype(jnp.bfloat16)
    grad_down = jnp.concatenate([jnp.moveaxis(total, 1, 0) for total in acc_down], axis=0).astype(jnp.bfloat16)
    return (grad_up, grad_down)
```

```python
import jax
import jax.numpy as jnp
from jax import lax
from jax.experimental import pallas as pl
from jax.experimental.pallas import tpu as pltpu
from jax.sharding import PartitionSpec as P

EPSILON = 1e-06
MESH = pl.DeviceIdType.MESH
F32 = jnp.float32
BF16 = jnp.bfloat16
EXPERTS = 32
GROUPS = 4
TOKENS = 256
MSG = 16
SLOTS = EXPERTS * MSG
PART = 896
HALF = 512
CHUNKS = 2
CROWS = SLOTS // CHUNKS
QUART = CROWS // GROUPS
CPEERS = EXPERTS // CHUNKS
VMEM_LIMIT = 56 * 1024 * 1024


def dot(a, b):
    return lax.dot_general(a, b, (((1,), (0,)), ((), ())), preferred_element_type=F32)


def dot_t(a, b):
    return lax.dot_general(a, b, (((1,), (1,)), ((), ())), preferred_element_type=F32)


def t_dot(a, b):
    return lax.dot_general(a, b, (((0,), (0,)), ((), ())), preferred_element_type=F32)


def copy_to(src, dst, send_sem, recv_sem, device):
    return pltpu.make_async_remote_copy(
        src_ref=src,
        dst_ref=dst,
        send_sem=send_sem,
        recv_sem=recv_sem,
        device_id=device,
        device_id_type=MESH,
    )


class Place:
    def __init__(self):
        self.section = lax.axis_index("section")
        self.expert = lax.axis_index("expert")
        self.group = lax.axis_index("dp")
        self.half = self.section % 2
        self.pair = self.section // 2
        self.partner = self.section + 1 - 2 * self.half


def greet_experts(here, barrier):
    def one(k, carry):
        pl.semaphore_signal(
            barrier,
            inc=1,
            device_id={"expert": (here.expert + k) % EXPERTS},
            device_id_type=MESH,
        )
        return carry

    lax.fori_loop(1, EXPERTS, one, 0)


def greet(barrier, device):
    pl.semaphore_signal(barrier, inc=1, device_id=device, device_id_type=MESH)


class Exchange:
    def __init__(self, here, src, dst, sems, sign):
        self.here, self.src, self.dst, self.sems, self.sign = here, src, dst, sems, sign

    def copy(self, k):
        rows = pl.ds(pl.multiple_of(k * MSG, MSG), MSG)
        peer = (self.here.expert + self.sign * k + EXPERTS) % EXPERTS
        return copy_to(
            self.src.at[rows],
            self.dst.at[rows],
            self.sems.at[0, k],
            self.sems.at[1, k],
            {"expert": peer},
        )

    def start(self, low=0, high=EXPERTS):
        if low == 0:
            self.dst[0:MSG] = self.src[0:MSG]

        def one(k, carry):
            self.copy(k).start()
            return carry

        lax.fori_loop(max(low, 1), high, one, 0)

    def wait_recv(self, low=0, high=EXPERTS):
        def one(k, carry):
            self.copy(k).wait_recv()
            return carry

        lax.fori_loop(max(low, 1), high, one, 0)

    def wait_send(self):
        def one(k, carry):
            self.copy(k).wait_send()
            return carry

        lax.fori_loop(1, EXPERTS, one, 0)


class GroupSum:
    def __init__(self, here, parts, landed, sems):
        self.here, self.parts, self.landed, self.sems = here, parts, landed, sems

    def copy(self, c, j):
        peer = (self.here.group + j) % GROUPS
        rows = pl.ds(pl.multiple_of(c * CROWS + peer * QUART, QUART), QUART)
        return copy_to(
            self.parts.at[rows],
            self.landed.at[c, j - 1],
            self.sems.at[0, c, j - 1],
            self.sems.at[1, c, j - 1],
            {"dp": peer},
        )

    def start(self, c):
        for j in (2, 1, 3):
            self.copy(c, j).start()

    def total(self, c):
        for j in (1, 3, 2):
            self.copy(c, j).wait_recv()
        rows = pl.ds(pl.multiple_of(c * CROWS + self.here.group * QUART, QUART), QUART)
        value = self.parts[rows].astype(F32)
        for j in (1, 2, 3):
            value = value + self.landed[c, j - 1].astype(F32)
        return value

    def wait_send(self):
        for c in range(CHUNKS):
            for j in (1, 2, 3):
                self.copy(c, j).wait_send()


class GroupGather:
    def __init__(self, here, whole, sems):
        self.here, self.whole, self.sems = here, whole, sems

    def rows(self, c, j):
        quarter = (self.here.group + GROUPS - j) % GROUPS
        return pl.ds(pl.multiple_of(c * CROWS + quarter * QUART, QUART), QUART)

    def copy(self, c, j, owner):
        where = self.whole.at[self.rows(c, owner)]
        return copy_to(
            where,
            where,
            self.sems.at[0, c, j - 1],
            self.sems.at[1, c, j - 1],
            {"dp": (self.here.group + j) % GROUPS},
        )

    def put(self, c, value):
        self.whole[self.rows(c, 0)] = value

    def start(self, c):
        for j in (2, 1, 3):
            self.copy(c, j, 0).start()

    def wait_recv(self, c):
        for j in (1, 3, 2):
            self.copy(c, j, j).wait_recv()

    def wait_send(self):
        for c in range(CHUNKS):
            for j in (1, 2, 3):
                self.copy(c, j, 0).wait_send()


class TokenSum:
    def __init__(self, here, own, landed, sems):
        self.here, self.own, self.landed, self.sems = here, own, landed, sems

    def copy(self, j):
        return copy_to(
            self.own,
            self.landed.at[j - 1],
            self.sems.at[0, j - 1],
            self.sems.at[1, j - 1],
            {"dp": (self.here.group + j) % GROUPS},
        )

    def start(self, column):
        self.own[...] = jnp.broadcast_to(column, (TOKENS, 128)).T[0:8]
        for j in (2, 1, 3):
            self.copy(j).start()

    def total(self):
        for j in (1, 3, 2):
            self.copy(j).wait_recv()
        value = self.own[...] + self.landed[0] + self.landed[1] + self.landed[2]
        return jnp.broadcast_to(value[0:1], (128, TOKENS)).T[:, 0:1]

    def wait_send(self):
        for j in (1, 2, 3):
            self.copy(j).wait_send()


def picks_by_slot(slot_row):
    slots = lax.broadcasted_iota(jnp.int32, (SLOTS, TOKENS), 0)
    return slots == slot_row[0:1], slots == slot_row[1:2]


def spread_of(slot_row):
    first, second = picks_by_slot(slot_row)
    return jnp.where(first | second, 1.0, 0.0).astype(BF16)


def shares_by_slot(slot_row, share_row):
    first, second = picks_by_slot(slot_row)
    return jnp.where(first, share_row[0:1], 0.0) + jnp.where(second, share_row[1:2], 0.0)


def picks_by_token(slot_col):
    slots = lax.broadcasted_iota(jnp.int32, (TOKENS, SLOTS), 1)
    return slots == slot_col[:, 0:1], slots == slot_col[:, 1:2]


def collect_of(slot_col):
    first, second = picks_by_token(slot_col)
    return jnp.where(first | second, 1.0, 0.0).astype(BF16)


def shares_by_token(slot_col, share_col):
    first, second = picks_by_token(slot_col)
    return jnp.where(first, share_col[:, 0:1], 0.0) + jnp.where(second, share_col[:, 1:2], 0.0)


def exact_dot(weights, values):
    high = weights.astype(BF16)
    low = (weights - high.astype(F32)).astype(BF16)
    return dot(high, values) + dot(low, values)


def up_parts(rows, up, up_other, parts, c):
    at = pl.ds(c * CROWS, CROWS)
    parts[at, 0:HALF] = dot(rows[at], up[...]).astype(BF16)
    parts[at, HALF:] = dot(rows[at], up_other[...]).astype(BF16)


def down_parts(rows, down, down_other, parts, c):
    at = pl.ds(c * CROWS, CROWS)
    parts[at, 0:HALF] = dot_t(rows[at], down[...]).astype(BF16)
    parts[at, HALF:] = dot_t(rows[at], down_other[...]).astype(BF16)


def norm_scale(total):
    return lax.rsqrt(total * (1.0 / (GROUPS * PART)) + EPSILON)


def pre_gradient(act_grad, pre):
    gate = jax.nn.sigmoid(pre)
    return (act_grad * gate * (1.0 + pre * (1.0 - gate))).astype(BF16)


def first_forward(
    stream, cotangent, up, down, gain, slot_row, slot_col, share_col,
    rows, pre, act, handed, cotan, up_other, down_other,
    layer_in, send, parts, landed, out, back, leaving, token_own, token_landed,
    stream_sems, cotan_sems, pair_sems, token_sems, go_sems, sum_sems, gather_sems, back_sems, hand_sems,
):
    here = Place()
    barrier = pltpu.get_barrier_semaphore()
    greet_experts(here, barrier)

    def greet_other(i, carry):
        at = (here.section * GROUPS + here.group + i) % 16
        greet(barrier, {"section": at // GROUPS, "dp": at % GROUPS})
        return carry

    lax.fori_loop(1, 16, greet_other, 0)
    pl.semaphore_wait(barrier, EXPERTS - 1 + 15)

    def cut_copy(source, target, sems, section, owner):
        return copy_to(
            source, target.at[owner], sems.at[0, section], sems.at[1, owner],
            {"section": section, "dp": here.section},
        )

    def send_cut(source, target, sems, flip):
        for section in range(4):
            direction = section // 2 if not flip else 1 - section // 2
            stays = (here.section == section) & (here.group == section)

            @pl.when(stays)
            def _():
                target[pl.ds(here.group, 1)] = source[direction : direction + 1]

            @pl.when(jnp.logical_not(stays))
            def _():
                cut_copy(source.at[direction], target, sems, section, here.group).start()

    def wait_cut(source, target, sems, recv):
        for i in range(4):
            if recv:
                stays = (here.section == here.group) & (here.group == i)
            else:
                stays = (here.section == i) & (here.group == i)

            @pl.when(jnp.logical_not(stays))
            def _():
                if recv:
                    cut_copy(source.at[0], target, sems, 0, i).wait_recv()
                else:
                    cut_copy(source.at[0], target, sems, i, here.group).wait_send()

    send_cut(stream, layer_in, stream_sems, False)
    to_partner = {"section": here.partner}
    up_copy = copy_to(up, up_other, pair_sems.at[0, 0], pair_sems.at[1, 0], to_partner)
    down_copy = copy_to(down, down_other, pair_sems.at[0, 1], pair_sems.at[1, 1], to_partner)
    up_copy.start()

    wait_cut(stream, layer_in, stream_sems, True)
    token_sum = TokenSum(here, token_own, token_landed, token_sems)
    values = layer_in[...].reshape(TOKENS, PART).astype(F32)
    token_sum.start(jnp.sum(values * values, axis=1, keepdims=True))
    spread = spread_of(slot_row[...])
    scale = norm_scale(token_sum.total())
    normed = (values * scale * gain[...]).astype(BF16)
    send[...] = dot(spread, normed).astype(BF16)
    go = Exchange(here, send, rows, go_sems, 1)
    go.start()
    down_copy.start()
    send_cut(cotangent, cotan, cotan_sems, True)

    group_sum = GroupSum(here, parts, landed, sum_sems)
    gather = GroupGather(here, act, gather_sems)
    go_back = Exchange(here, out, back, back_sems, -1)
    up_copy.wait_recv()
    for c in range(CHUNKS):
        go.wait_recv(c * CPEERS, (c + 1) * CPEERS)
        up_parts(rows, up, up_other, parts, c)
        group_sum.start(c)
    for c in range(CHUNKS):
        total = group_sum.total(c)
        pre[c] = total
        gather.put(c, (total * jax.nn.sigmoid(total)).astype(BF16))
        gather.start(c)
    down_copy.wait_recv()
    for c in range(CHUNKS):
        gather.wait_recv(c)
        at = pl.ds(c * CROWS, CROWS)
        made = dot(act[at, 0:HALF], down[...]) + dot(act[at, HALF:], down_other[...])
        out[at] = made.astype(BF16)
        go_back.start(c * CPEERS, (c + 1) * CPEERS)
    weights = shares_by_token(slot_col[...], share_col[...])
    go_back.wait_recv()
    residual = layer_in[...].reshape(TOKENS, PART).astype(F32) * (1 - here.half).astype(F32)
    leaving[...] = (residual + exact_dot(weights, back[...])).astype(BF16)
    hand_on(here, leaving, handed, hand_sems)

    wait_cut(cotangent, cotan, cotan_sems, True)
    wait_cut(stream, layer_in, stream_sems, False)
    wait_cut(cotangent, cotan, cotan_sems, False)
    up_copy.wait_send()
    down_copy.wait_send()
    token_sum.wait_send()
    go.wait_send()
    group_sum.wait_send()
    gather.wait_send()
    go_back.wait_send()


def hand_on(here, leaving, handed, sems):
    def one(j, owner):
        return copy_to(
            leaving, handed.at[owner], sems.at[0, j], sems.at[1, owner],
            {"section": 2 * (1 - here.pair) + j},
        )

    for j in range(2):
        one(j, here.half).start()
    for j in range(2):
        one(0, j).wait_recv()
    for j in range(2):
        one(j, here.half).wait_send()


def greet_near(here, barrier, other_pair, partner):
    greet_experts(here, barrier)
    for j in (1, 2, 3):
        greet(barrier, {"dp": (here.group + j) % GROUPS})
    count = EXPERTS - 1 + 3
    if other_pair:
        for j in range(2):
            greet(barrier, {"section": 2 * (1 - here.pair) + j})
        count += 2
    if partner:
        greet(barrier, {"section": here.partner})
        count += 1
    pl.semaphore_wait(barrier, count)


def second_layer(
    handed, cotan, up, up_other, down, down_other, gain, slot_row, slot_col, share_row,
    rows, act, grads, pre_grad, handed_back,
    send, send_grads, parts, landed, grad_parts, grad_landed, out, back, leaving,
    token_own, token_landed, mix_own, mix_landed,
    token_sems, mix_sems, go_sems, grad_sems, sum_sems, grad_sum_sems, gather_sems, act_sems, back_sems, hand_sems,
):
    here = Place()
    greet_near(here, pltpu.get_barrier_semaphore(), True, False)

    def layer_in():
        return (handed[0].astype(F32) + handed[1].astype(F32)).astype(BF16).astype(F32)

    token_sum = TokenSum(here, token_own, token_landed, token_sems)
    values = layer_in()
    token_sum.start(jnp.sum(values * values, axis=1, keepdims=True))
    spread = spread_of(slot_row[...])
    shares = shares_by_slot(slot_row[...], share_row[...])
    send_grads[...] = exact_dot(shares, cotan[...].reshape(TOKENS, PART)).astype(BF16)
    scale = norm_scale(token_sum.total())
    normed = (layer_in() * scale * gain[...]).astype(BF16)
    send[...] = dot(spread, normed).astype(BF16)
    go = Exchange(here, send, rows, go_sems, 1)
    go_grads = Exchange(here, send_grads, grads, grad_sems, 1)
    go.start()
    go_grads.start()

    group_sum = GroupSum(here, parts, landed, sum_sems)
    grad_sum = GroupSum(here, grad_parts, grad_landed, grad_sum_sems)
    gather = GroupGather(here, pre_grad, gather_sems)
    act_gather = GroupGather(here, act, act_sems)
    go_back = Exchange(here, out, back, back_sems, -1)
    for c in range(CHUNKS):
        go.wait_recv(c * CPEERS, (c + 1) * CPEERS)
        up_parts(rows, up, up_other, parts, c)
        group_sum.start(c)
    for c in range(CHUNKS):
        go_grads.wait_recv(c * CPEERS, (c + 1) * CPEERS)
        down_parts(grads, down, down_other, grad_parts, c)
        grad_sum.start(c)
    for c in range(CHUNKS):
        pre = group_sum.total(c)
        act_gather.put(c, (pre * jax.nn.sigmoid(pre)).astype(BF16))
        gather.put(c, pre_gradient(grad_sum.total(c), pre))
        gather.start(c)
    for c in range(CHUNKS):
        gather.wait_recv(c)
        at = pl.ds(c * CROWS, CROWS)
        made = dot_t(pre_grad[at, 0:HALF], up[...]) + dot_t(pre_grad[at, HALF:], up_other[...])
        out[at] = made.astype(BF16)
        go_back.start(c * CPEERS, (c + 1) * CPEERS)
    for c in range(CHUNKS):
        act_gather.start(c)
    collect = collect_of(slot_col[...])
    go_back.wait_recv()
    scaled = dot(collect, back[...]) * gain[...]
    mix = TokenSum(here, mix_own, mix_landed, mix_sems)
    mix.start(jnp.sum(layer_in() * scaled, axis=1, keepdims=True))
    direct = cotan[...].reshape(TOKENS, PART).astype(F32) * (1 - here.half).astype(F32)
    direct = direct + scale * scaled
    mean = mix.total() * (1.0 / (GROUPS * PART))
    leaving[...] = (direct - layer_in() * (scale * scale * scale * mean)).astype(BF16)
    hand_on(here, leaving, handed_back, hand_sems)

    for c in range(CHUNKS):
        act_gather.wait_recv(c)
    token_sum.wait_send()
    mix.wait_send()
    go.wait_send()
    go_grads.wait_send()
    group_sum.wait_send()
    grad_sum.wait_send()
    gather.wait_send()
    act_gather.wait_send()
    go_back.wait_send()


def first_backward(
    handed_back, down, down_other, slot_row, share_row, rows1, act1, pre1, rows2, act2, grads2, pre_grad2,
    grad_up, grad_down,
    send, grads1, pre_grad1, parts, landed, sum_up, sum_down, give_up, give_down, got_up, got_down,
    go_sems, sum_sems, gather_sems, pair_sems,
):
    here = Place()
    greet_near(here, pltpu.get_barrier_semaphore(), False, True)
    incoming = (handed_back[0].astype(F32) + handed_back[1].astype(F32)).astype(BF16)
    send[...] = exact_dot(shares_by_slot(slot_row[...], share_row[...]), incoming).astype(BF16)
    go = Exchange(here, send, grads1, go_sems, 1)
    go.start()

    @pl.loop(0, PART // 128)
    def _(i):
        at = pl.ds(pl.multiple_of(i * 128, 128), 128)
        sum_up[at] = t_dot(rows2[:, at], pre_grad2[...])

    @pl.loop(0, 2 * HALF // 128)
    def _(i):
        at = pl.ds(pl.multiple_of(i * 128, 128), 128)
        sum_down[at] = t_dot(act2[:, at], grads2[...])

    group_sum = GroupSum(here, parts, landed, sum_sems)
    gather = GroupGather(here, pre_grad1, gather_sems)
    to_partner = {"section": here.partner}
    down_copy = copy_to(give_down, got_down, pair_sems.at[0, 0], pair_sems.at[1, 0], to_partner)
    up_copy = copy_to(give_up, got_up, pair_sems.at[0, 1], pair_sems.at[1, 1], to_partner)
    for c in range(CHUNKS):
        go.wait_recv(c * CPEERS, (c + 1) * CPEERS)
        down_parts(grads1, down, down_other, parts, c)
        group_sum.start(c)

    @pl.loop(0, HALF // 128)
    def _(i):
        at = pl.ds(pl.multiple_of(i * 128, 128), 128)
        far = pl.ds(pl.multiple_of(HALF + i * 128, 128), 128)
        give_down[at] = (sum_down[far] + t_dot(act1[:, far], grads1[...])).astype(BF16)

    down_copy.start()
    for c in range(CHUNKS):
        gather.put(c, pre_gradient(group_sum.total(c), pre1[c]))
        gather.start(c)

    @pl.loop(0, HALF // 128)
    def _(i):
        at = pl.ds(pl.multiple_of(i * 128, 128), 128)
        sum_down[at] += t_dot(act1[:, at], grads1[...])

    for c in range(CHUNKS):
        gather.wait_recv(c)

    @pl.loop(0, PART // 128)
    def _(i):
        at = pl.ds(pl.multiple_of(i * 128, 128), 128)
        give_up[at] = (sum_up[at, HALF:] + t_dot(rows1[:, at], pre_grad1[:, HALF:])).astype(BF16)

    up_copy.start()

    @pl.loop(0, PART // 128)
    def _(i):
        at = pl.ds(pl.multiple_of(i * 128, 128), 128)
        sum_up[at, 0:HALF] += t_dot(rows1[:, at], pre_grad1[:, 0:HALF])

    down_copy.wait_recv()
    grad_down[...] = (sum_down[0:HALF] + got_down[...].astype(F32)).astype(BF16)
    up_copy.wait_recv()
    grad_up[...] = (sum_up[:, 0:HALF] + got_up[...].astype(F32)).astype(BF16)
    down_copy.wait_send()
    up_copy.wait_send()
    go.wait_send()
    group_sum.wait_send()
    gather.wait_send()


def call(kernel, collective_id, outs, scratch, *operands):
    whole = pl.BlockSpec(memory_space=pltpu.VMEM)
    return pl.pallas_call(
        kernel,
        out_shape=[jax.ShapeDtypeStruct(shape, dtype) for shape, dtype in outs],
        in_specs=[whole] * len(operands),
        out_specs=[whole] * len(outs),
        scratch_shapes=scratch,
        compiler_params=pltpu.CompilerParams(
            collective_id=collective_id, has_side_effects=True, vmem_limit_bytes=VMEM_LIMIT
        ),
    )(*operands)


def routing(route_ids, route_gates, pair, half):
    ids = lax.dynamic_index_in_dim(route_ids, pair, 0, keepdims=False)
    gates = lax.dynamic_index_in_dim(route_gates, pair, 0, keepdims=False)
    shares = gates / jnp.sum(gates, axis=-1, keepdims=True)
    ids, shares = (jnp.where(pair == 0, value, value[::-1]) for value in (ids, shares))
    uses, batches, tokens, top = ids.shape
    flat = ids.reshape(uses, batches, tokens * top)
    before = jnp.tri(tokens * top, k=-1, dtype=jnp.bool_)
    position = jnp.sum((flat[..., :, None] == flat[..., None, :]) & before, axis=-1)
    away = (flat - lax.axis_index("expert") + EXPERTS) % EXPERTS
    batch = jnp.arange(batches, dtype=jnp.int32)[None, :, None]
    slot = away * MSG + batch * (MSG // 2) + lax.axis_index("dp") * 2 + position % 2
    slot = jnp.where(position // 2 == half, slot, -1)
    both = jnp.stack([slot.astype(F32).reshape(ids.shape), shares], axis=-1)
    both = both.reshape(uses, batches * tokens, top, 2)
    both = lax.all_gather(both, "dp", axis=1, tiled=True)
    slots, shares = both[..., 0].astype(jnp.int32), both[..., 1]
    return slots, shares


def local(stream_in, cotangent, route_ids, route_gates, norm_gain, up_weight, down_weight):
    section = lax.axis_index("section")
    pair, half = section // 2, section % 2
    slots, shares = routing(route_ids, route_gates, pair, half)
    slot_rows, share_rows = slots.transpose(0, 2, 1), shares.transpose(0, 2, 1)
    gain = lax.dynamic_slice(norm_gain, (pair, lax.axis_index("dp") * PART), (1, PART))
    up, down = up_weight[0, 0], down_weight[0, 0]

    dma = pltpu.SemaphoreType.DMA
    hidden, features = ((SLOTS, 2 * HALF), BF16), ((SLOTS, PART), BF16)
    tokens, quarter = ((GROUPS, 2, 32, PART), BF16), ((CHUNKS, QUART, 2 * HALF), F32)
    handed_shape = ((2, TOKENS, PART), BF16)
    vm_hidden, vm_features = pltpu.VMEM(*hidden), pltpu.VMEM(*features)
    vm_landed = pltpu.VMEM((CHUNKS, 3, QUART, 2 * HALF), BF16)
    vm_leaving = pltpu.VMEM((TOKENS, PART), BF16)
    vm_token = [pltpu.VMEM((8, TOKENS), F32), pltpu.VMEM((3, 8, TOKENS), F32)]
    sem_group, sem_peers = dma((2, CHUNKS, 3)), dma((2, EXPERTS))

    rows1, pre1, act1, handed, cotan, up_other, down_other = call(
        first_forward,
        0,
        [features, quarter, hidden, handed_shape, tokens, ((PART, HALF), BF16), ((HALF, PART), BF16)],
        [pltpu.VMEM(*tokens), vm_features, vm_hidden, vm_landed, vm_features, vm_features, vm_leaving, *vm_token]
        + [dma((2, 4)), dma((2, 4)), dma((2, 2)), dma((2, 3)), sem_peers]
        + [sem_group, sem_group, sem_peers, dma((2, 2))],
        stream_in, cotangent, up, down, gain, slot_rows[0], slots[0], shares[0],
    )
    rows2, act2, grads2, pre_grad2, handed_back = call(
        second_layer,
        1,
        [features, hidden, features, hidden, handed_shape],
        [vm_features, vm_features, vm_hidden, vm_landed, vm_hidden, vm_landed, vm_features, vm_features, vm_leaving]
        + [*vm_token, *vm_token, dma((2, 3)), dma((2, 3)), sem_peers, sem_peers]
        + [sem_group, sem_group, sem_group, sem_group, sem_peers, dma((2, 2))],
        handed, cotan, up, up_other, down, down_other, gain, slot_rows[1], slots[1], share_rows[1],
    )
    grad_up, grad_down = call(
        first_backward,
        2,
        [((PART, HALF), BF16), ((HALF, PART), BF16)],
        [vm_features, vm_features, vm_hidden, vm_hidden, vm_landed]
        + [pltpu.VMEM((PART, 2 * HALF), F32), pltpu.VMEM((2 * HALF, PART), F32)]
        + [pltpu.VMEM((PART, HALF), BF16), pltpu.VMEM((HALF, PART), BF16)] * 2
        + [sem_peers, sem_group, sem_group, dma((2, 2))],
        handed_back, down, down_other, slot_rows[0], share_rows[0],
        rows1, act1, pre1, rows2, act2, grads2, pre_grad2,
    )
    return grad_up[None, None], grad_down[None, None]


def solution(mesh):
    placed = (
        P(None, None, ("expert", "dp"), "section"),
        P(None, None, ("expert", "dp"), "section"),
        P(None, None, None, ("expert", "dp"), None),
        P(None, None, None, ("expert", "dp"), None),
        P(),
        P("section", "expert", "dp", None),
        P("section", "expert", None, "dp"),
    )
    return jax.shard_map(
        local,
        mesh=mesh,
        in_specs=placed,
        out_specs=(P("section", "expert", "dp", None), P("section", "expert", None, "dp")),
        check_vma=False,
    )
```

```python
import jax
import jax.numpy as jnp
from jax import lax
from jax.experimental import pallas as pl
from jax.experimental.pallas import tpu as pltpu
from jax.sharding import PartitionSpec as P

EPSILON = 1e-06
MESH = pl.DeviceIdType.MESH
F32 = jnp.float32
BF16 = jnp.bfloat16
EXPERTS = 32
GROUPS = 4
BATCHES = 2
BLOCK = 32
TOKENS = GROUPS * BLOCK
MSG = 8
SLOTS = EXPERTS * MSG
QUART = SLOTS // GROUPS
PART = 896
HALF = 512
VMEM_LIMIT = 56 * 1024 * 1024


def dot(a, b):
    return lax.dot_general(a, b, (((1,), (0,)), ((), ())), preferred_element_type=F32)


def dot_t(a, b):
    return lax.dot_general(a, b, (((1,), (1,)), ((), ())), preferred_element_type=F32)


def t_dot(a, b):
    return lax.dot_general(a, b, (((0,), (0,)), ((), ())), preferred_element_type=F32)


def copy_to(src, dst, send_sem, recv_sem, device):
    return pltpu.make_async_remote_copy(
        src_ref=src,
        dst_ref=dst,
        send_sem=send_sem,
        recv_sem=recv_sem,
        device_id=device,
        device_id_type=MESH,
    )


class Place:
    def __init__(self):
        self.section = lax.axis_index("section")
        self.expert = lax.axis_index("expert")
        self.group = lax.axis_index("dp")
        self.half = self.section % 2
        self.pair = self.section // 2
        self.partner = self.section + 1 - 2 * self.half


def greet_experts(here, barrier):
    def one(k, carry):
        pl.semaphore_signal(
            barrier,
            inc=1,
            device_id={"expert": (here.expert + k) % EXPERTS},
            device_id_type=MESH,
        )
        return carry

    lax.fori_loop(1, EXPERTS, one, 0)


def greet(barrier, device):
    pl.semaphore_signal(barrier, inc=1, device_id=device, device_id_type=MESH)


class Exchange:
    def __init__(self, here, src, dst, sems, sign):
        self.here, self.src, self.dst, self.sems, self.sign = here, src, dst, sems, sign

    def copy(self, k, count=1):
        which = pl.ds(k, count)
        peer = (self.here.expert + self.sign * k + EXPERTS) % EXPERTS
        return copy_to(
            self.src.at[which], self.dst.at[which], self.sems.at[0], self.sems.at[1], {"expert": peer}
        )

    def start(self, rows):
        messages = rows.reshape(EXPERTS, MSG, PART).astype(BF16)
        self.src[...] = messages
        self.dst[0:1] = messages[0:1]

        def one(k, carry):
            self.copy(k).start()
            return carry

        lax.fori_loop(1, EXPERTS, one, 0)

    def take(self):
        self.copy(1, EXPERTS - 1).wait_recv()
        return self.dst[...].astype(F32).reshape(SLOTS, PART).astype(BF16)

    def wait_send(self):
        self.copy(1, EXPERTS - 1).wait_send()


class GroupSum:
    def __init__(self, here, parts, landed, sems):
        self.here, self.parts, self.landed, self.sems = here, parts, landed, sems

    def copy(self, j):
        peer = (self.here.group + j) % GROUPS
        rows = pl.ds(pl.multiple_of(peer * QUART, QUART), QUART)
        return copy_to(
            self.parts.at[rows],
            self.landed.at[j - 1],
            self.sems.at[0, j - 1],
            self.sems.at[1, j - 1],
            {"dp": peer},
        )

    def start(self, near, far):
        self.parts[:, 0:HALF] = near.astype(BF16)
        self.parts[:, HALF:] = far.astype(BF16)
        for j in (2, 1, 3):
            self.copy(j).start()

    def total(self):
        for j in (1, 3, 2):
            self.copy(j).wait_recv()
        rows = pl.ds(pl.multiple_of(self.here.group * QUART, QUART), QUART)
        value = self.parts[rows].astype(F32)
        for j in (1, 2, 3):
            value = value + self.landed[j - 1].astype(F32)
        return value

    def wait_send(self):
        for j in (1, 2, 3):
            self.copy(j).wait_send()


class GroupGather:
    def __init__(self, here, whole, sems):
        self.here, self.whole, self.sems = here, whole, sems

    def rows(self, back):
        quarter = (self.here.group + GROUPS - back) % GROUPS
        return pl.ds(pl.multiple_of(quarter * QUART, QUART), QUART)

    def copy(self, to, back, half, slot):
        where = self.whole.at[self.rows(back), pl.ds(half * HALF, HALF)]
        return copy_to(
            where, where, self.sems.at[0, slot], self.sems.at[1, slot],
            {"dp": (self.here.group + to) % GROUPS},
        )

    def start(self, value):
        self.whole[self.rows(0)] = value
        for slot, (to, half) in enumerate(((1, 0), (3, 1), (1, 1), (3, 0))):
            self.copy(to, 0, half, slot).start()

    def pass_on(self):
        self.copy(1, 1, 0, 0).wait_recv()
        self.copy(1, 1, 0, 4).start()
        self.copy(3, 3, 1, 1).wait_recv()
        self.copy(3, 3, 1, 5).start()

    def wait_recv(self):
        self.copy(1, 1, 1, 2).wait_recv()
        self.copy(3, 3, 0, 3).wait_recv()
        self.copy(1, 2, 0, 4).wait_recv()
        self.copy(3, 2, 1, 5).wait_recv()

    def wait_send(self):
        for slot, (to, half) in enumerate(((1, 0), (3, 1), (1, 1), (3, 0))):
            self.copy(to, 0, half, slot).wait_send()
        self.copy(1, 1, 0, 4).wait_send()
        self.copy(3, 3, 1, 5).wait_send()


class SmallSum:
    def __init__(self, here, own, landed, sems):
        self.here, self.own, self.landed, self.sems = here, own, landed, sems

    def copy(self, j):
        return copy_to(
            self.own,
            self.landed.at[j - 1],
            self.sems.at[0, j - 1],
            self.sems.at[1, j - 1],
            {"dp": (self.here.group + j) % GROUPS},
        )

    def start(self):
        for j in (2, 1, 3):
            self.copy(j).start()

    def start_column(self, column):
        self.own[...] = jnp.broadcast_to(column, (TOKENS, TOKENS)).T[0:8]
        self.start()

    def total(self):
        for j in (1, 3, 2):
            self.copy(j).wait_recv()
        return self.own[...] + self.landed[0] + self.landed[1] + self.landed[2]

    def total_column(self):
        return jnp.broadcast_to(self.total()[0:1], (TOKENS, TOKENS)).T[:, 0:1]

    def wait_send(self):
        for j in (1, 2, 3):
            self.copy(j).wait_send()


class HandOn:
    def __init__(self, here, leaving, handed, sems):
        self.here, self.leaving, self.handed, self.sems = here, leaving, handed, sems

    def copy(self, to, owner):
        return copy_to(
            self.leaving, self.handed.at[owner], self.sems.at[0, to], self.sems.at[1, owner],
            {"section": 2 * (1 - self.here.pair) + to},
        )

    def start(self, value):
        self.leaving[...] = value.astype(BF16)
        for to in range(2):
            self.copy(to, self.here.half).start()

    def take(self):
        for owner in range(2):
            self.copy(0, owner).wait_recv()
        return (self.handed[0].astype(F32) + self.handed[1].astype(F32)).astype(BF16)

    def again(self):
        return (self.handed[0].astype(F32) + self.handed[1].astype(F32)).astype(BF16)

    def wait_send(self):
        for to in range(2):
            self.copy(to, self.here.half).wait_send()


class Cut:
    def __init__(self, here, source, target, sems, flip):
        self.here, self.source, self.target, self.sems, self.flip = here, source, target, sems, flip

    def copy(self, m, section, owner):
        direction = 1 - section // 2 if self.flip else section // 2
        return copy_to(
            self.source.at[direction, m], self.target.at[m, owner],
            self.sems.at[0, m, section], self.sems.at[1, m, owner],
            {"section": section, "dp": self.here.section},
        )

    def start(self, m):
        for section in range(4):
            direction = 1 - section // 2 if self.flip else section // 2
            stays = (self.here.section == section) & (self.here.group == section)

            @pl.when(stays)
            def _():
                self.target[m, pl.ds(self.here.group, 1)] = self.source[direction, m : m + 1]

            @pl.when(jnp.logical_not(stays))
            def _():
                self.copy(m, section, self.here.group).start()

    def take(self, m):
        for owner in range(4):
            stays = (self.here.section == self.here.group) & (self.here.group == owner)

            @pl.when(jnp.logical_not(stays))
            def _():
                self.copy(m, 0, owner).wait_recv()

    def value(self, m):
        return self.target[m].reshape(TOKENS, PART)

    def wait_send(self):
        for m in range(BATCHES):
            for section in range(4):
                stays = (self.here.section == section) & (self.here.group == section)

                @pl.when(jnp.logical_not(stays))
                def _():
                    self.copy(m, section, self.here.group).wait_send()


class Routes:
    def __init__(self, rows, columns):
        self.rows, self.columns = rows, columns

    def by_slot(self, u, m):
        slots = lax.broadcasted_iota(jnp.int32, (SLOTS, TOKENS), 0).astype(F32)
        at = m * 8 + u * 4
        return [(slots == self.rows[at + 2 * k : at + 2 * k + 1], self.rows[at + 2 * k + 1 : at + 2 * k + 2]) for k in range(2)]

    def by_token(self, u, m):
        slots = lax.broadcasted_iota(jnp.int32, (TOKENS, SLOTS), 1).astype(F32)
        at = m * 8 + u * 4
        return [(slots == self.columns[:, at + 2 * k : at + 2 * k + 1], self.columns[:, at + 2 * k + 1 : at + 2 * k + 2]) for k in range(2)]


def marks(picks):
    (first, _), (second, _) = picks
    return jnp.where(first | second, 1.0, 0.0).astype(BF16)


def weighted(picks):
    (first, share), (second, other) = picks
    return jnp.where(first, share, 0.0) + jnp.where(second, other, 0.0)


def exact_dot(weights, values):
    high = weights.astype(BF16)
    low = (weights - high.astype(F32)).astype(BF16)
    return dot(high, values) + dot(low, values)


def norm_scale(total):
    return lax.rsqrt(total * (1.0 / (GROUPS * PART)) + EPSILON)


def silu(pre):
    return pre * jax.nn.sigmoid(pre)


def pre_gradient(act_grad, pre):
    gate = jax.nn.sigmoid(pre)
    return (act_grad * gate * (1.0 + pre * (1.0 - gate))).astype(BF16)


def row_sum(values):
    return jnp.sum(values, axis=1, keepdims=True)


def update(
    stream, cotangent, up, down, norm_gain, routes_own,
    grad_up, grad_down,
    layer_in, cotan, up_other, down_other, routes_landed, routes_rows, routes_columns,
    sent, came, rows1, rows2, grads1, grads2, parts, landed, gathered, pre1, pre2,
    small_own, small_landed, scales, leaving, handed,
    sum_up, sum_down, give_up, give_down, got_up, got_down,
    cut_sems, pair_sems, route_sems, small_sems, peer_sems, sum_sems, gather_sems, hand_sems,
):
    here = Place()
    both = range(BATCHES)
    barrier = pltpu.get_barrier_semaphore()
    greet_experts(here, barrier)

    def greet_other(i, carry):
        at = (here.section * GROUPS + here.group + i) % 16
        greet(barrier, {"section": at // GROUPS, "dp": at % GROUPS})
        return carry

    lax.fori_loop(1, 16, greet_other, 0)
    pl.semaphore_wait(barrier, EXPERTS - 1 + 15)

    def exchanges(i, sign):
        return [Exchange(here, sent.at[i, m], came.at[i, m], peer_sems.at[i, m], sign) for m in both]

    go1, back1, go_grads, go2, back2, go3 = (
        exchanges(i, sign) for i, sign in enumerate((1, -1, 1, 1, -1, 1))
    )
    sum1, sum2, sum_grads2, sum_grads1 = (
        [GroupSum(here, parts.at[i, m], landed.at[i, m], sum_sems.at[i, m]) for m in both] for i in range(4)
    )
    act1, act2, pre_grad2, pre_grad1 = ([gathered.at[i, m] for m in both] for i in range(4))
    all_act1, all_act2, all_pre_grad2, all_pre_grad1 = (
        [GroupGather(here, gathered.at[i, m], gather_sems.at[i, m]) for m in both] for i in range(4)
    )
    norm1, norm2, mix = (
        [SmallSum(here, small_own.at[i, m], small_landed.at[i, m], small_sems.at[i, m]) for m in both]
        for i in range(3)
    )
    hand1, hand2 = (
        [HandOn(here, leaving.at[i, m], handed.at[i, m], hand_sems.at[i, m]) for m in both] for i in range(2)
    )
    cut_in = Cut(here, stream, layer_in, cut_sems.at[0], False)
    cut_cotan = Cut(here, cotangent, cotan, cut_sems.at[1], True)
    route_sum = SmallSum(here, routes_own, routes_landed, route_sems)
    routes = Routes(routes_rows, routes_columns)
    to_partner = {"section": here.partner}

    def pair_copy(i, source, target):
        return copy_to(source, target, pair_sems.at[0, i], pair_sems.at[1, i], to_partner)

    up_copy, down_copy = pair_copy(0, up, up_other), pair_copy(1, down, down_other)
    give_down_copy, give_up_copy = pair_copy(2, give_down, got_down), pair_copy(3, give_up, got_up)
    gain = norm_gain[pl.ds(here.pair, 1), pl.ds(pl.multiple_of(here.group * PART, PART), PART)]
    first_half = (1 - here.half).astype(F32)

    def up_parts(rows, target):
        target.start(dot(rows[...], up[...]), dot(rows[...], up_other[...]))

    def down_parts(rows, target):
        target.start(dot_t(rows[...], down[...]), dot_t(rows[...], down_other[...]))

    route_sum.start()
    for m in both:
        cut_in.start(m)
    up_copy.start()
    for m in both:
        cut_in.take(m)
        values = cut_in.value(m).astype(F32)
        norm1[m].start_column(row_sum(values * values))
    total = route_sum.total()
    routes_rows[...] = total
    routes_columns[...] = jnp.concatenate([total] * (TOKENS // total.shape[0]), axis=0).T
    for m in both:
        scale = norm_scale(norm1[m].total_column())
        normed = (cut_in.value(m).astype(F32) * scale * gain).astype(BF16)
        go1[m].start(dot(marks(routes.by_slot(0, m)), normed))
    down_copy.start()
    for m in both:
        cut_cotan.start(m)
    up_copy.wait_recv()
    for m in both:
        rows1[m] = go1[m].take()
        up_parts(rows1.at[m], sum1[m])
    for m in both:
        cut_cotan.take(m)
        go_grads[m].start(exact_dot(weighted(routes.by_slot(1, m)), cut_cotan.value(m)))
    for m in both:
        pre1[m] = sum1[m].total()
        all_act1[m].start(silu(pre1[m]).astype(BF16))
    for m in both:
        all_act1[m].pass_on()
    down_copy.wait_recv()
    for m in both:
        all_act1[m].wait_recv()
        act = act1[m]
        back1[m].start(dot(act[:, 0:HALF], down[...]) + dot(act[:, HALF:], down_other[...]))
    for m in both:
        grads2[m] = go_grads[m].take()
        down_parts(grads2.at[m], sum_grads2[m])
    for m in both:
        expert_out = back1[m].take()
        direct = cut_in.value(m).astype(F32) * first_half
        hand1[m].start(direct + exact_dot(weighted(routes.by_token(0, m)), expert_out))

    for m in both:
        values = hand1[m].take().astype(F32)
        norm2[m].start_column(row_sum(values * values))
        scales[m] = norm_scale(norm2[m].total_column())
        normed = (hand1[m].again().astype(F32) * scales[m] * gain).astype(BF16)
        go2[m].start(dot(marks(routes.by_slot(1, m)), normed))
    for m in both:
        rows2[m] = go2[m].take()
        up_parts(rows2.at[m], sum2[m])
    for m in both:
        pre2[m] = sum2[m].total()
        all_pre_grad2[m].start(pre_gradient(sum_grads2[m].total(), pre2[m]))
    for m in both:
        all_pre_grad2[m].pass_on()
    for m in both:
        all_pre_grad2[m].wait_recv()
        grad = pre_grad2[m]
        back2[m].start(dot_t(grad[:, 0:HALF], up[...]) + dot_t(grad[:, HALF:], up_other[...]))
    for m in both:
        all_act2[m].start(silu(pre2[m]).astype(BF16))

    @pl.loop(0, PART // 128)
    def _(i):
        at = pl.ds(pl.multiple_of(i * 128, 128), 128)
        sum_up[at] = t_dot(rows2[0, :, at], pre_grad2[0][...]) + t_dot(rows2[1, :, at], pre_grad2[1][...])

    for m in both:
        scaled = dot(marks(routes.by_token(1, m)), back2[m].take()) * gain
        mix[m].start_column(row_sum(hand1[m].again().astype(F32) * scaled))
        direct = cut_cotan.value(m).astype(F32) * first_half + scales[m] * scaled
        mean = mix[m].total_column() * (1.0 / (GROUPS * PART))
        scale = scales[m]
        hand2[m].start(direct - hand1[m].again().astype(F32) * (scale * scale * scale * mean))
    for m in both:
        all_act2[m].pass_on()
    for m in both:
        all_act2[m].wait_recv()

    @pl.loop(0, 2 * HALF // 128)
    def _(i):
        at = pl.ds(pl.multiple_of(i * 128, 128), 128)
        sum_down[at] = t_dot(act2[0][:, at], grads2[0]) + t_dot(act2[1][:, at], grads2[1])

    for m in both:
        incoming = hand2[m].take()
        go3[m].start(exact_dot(weighted(routes.by_slot(0, m)), incoming))
    for m in both:
        grads1[m] = go3[m].take()
        down_parts(grads1.at[m], sum_grads1[m])

    @pl.loop(0, HALF // 128)
    def _(i):
        at = pl.ds(pl.multiple_of(i * 128, 128), 128)
        far = pl.ds(pl.multiple_of(HALF + i * 128, 128), 128)
        value = sum_down[far] + t_dot(act1[0][:, far], grads1[0]) + t_dot(act1[1][:, far], grads1[1])
        give_down[at] = value.astype(BF16)

    give_down_copy.start()
    for m in both:
        all_pre_grad1[m].start(pre_gradient(sum_grads1[m].total(), pre1[m]))
    for m in both:
        all_pre_grad1[m].pass_on()

    @pl.loop(0, HALF // 128)
    def _(i):
        at = pl.ds(pl.multiple_of(i * 128, 128), 128)
        sum_down[at] += t_dot(act1[0][:, at], grads1[0]) + t_dot(act1[1][:, at], grads1[1])

    for m in both:
        all_pre_grad1[m].wait_recv()

    @pl.loop(0, PART // 128)
    def _(i):
        at = pl.ds(pl.multiple_of(i * 128, 128), 128)
        value = sum_up[at, HALF:]
        for m in both:
            value = value + t_dot(rows1[m, :, at], pre_grad1[m][:, HALF:])
        give_up[at] = value.astype(BF16)

    give_up_copy.start()

    @pl.loop(0, PART // 128)
    def _(i):
        at = pl.ds(pl.multiple_of(i * 128, 128), 128)
        for m in both:
            sum_up[at, 0:HALF] += t_dot(rows1[m, :, at], pre_grad1[m][:, 0:HALF])

    give_down_copy.wait_recv()
    grad_down[...] = (sum_down[0:HALF] + got_down[...].astype(F32)).astype(BF16)
    give_up_copy.wait_recv()
    grad_up[...] = (sum_up[:, 0:HALF] + got_up[...].astype(F32)).astype(BF16)

    for sender in (cut_in, cut_cotan, route_sum, up_copy, down_copy, give_down_copy, give_up_copy):
        sender.wait_send()
    for senders in (go1, back1, go_grads, go2, back2, go3, sum1, sum2, sum_grads2, sum_grads1, all_act1,
                    all_act2, all_pre_grad2, all_pre_grad1, norm1, norm2, mix, hand1, hand2):
        for m in both:
            senders[m].wait_send()


def routing(route_ids, route_gates, pair, half):
    ids = lax.dynamic_index_in_dim(route_ids, pair, 0, keepdims=False)
    gates = lax.dynamic_index_in_dim(route_gates, pair, 0, keepdims=False)
    shares = gates / jnp.sum(gates, axis=-1, keepdims=True)
    ids, shares = (jnp.where(pair == 0, value, value[::-1]) for value in (ids, shares))
    uses, batches, tokens, top = ids.shape
    flat = ids.reshape(uses, batches, tokens * top)
    before = jnp.tri(tokens * top, k=-1, dtype=jnp.bool_)
    position = jnp.sum((flat[..., :, None] == flat[..., None, :]) & before, axis=-1)
    away = (flat - lax.axis_index("expert") + EXPERTS) % EXPERTS
    group = lax.axis_index("dp")
    slot = away * MSG + group * 2 + position % 2
    slot = jnp.where(position // 2 == half, slot, -1).astype(F32).reshape(ids.shape)
    values = jnp.stack([slot, shares], axis=-1).transpose(1, 0, 3, 4, 2).reshape(batches * uses * top * 2, tokens)
    lanes = jnp.arange(TOKENS, dtype=jnp.int32)[None, :] // BLOCK
    return jnp.where(lanes == group, jnp.tile(values, (1, GROUPS)), 0.0)


def local(stream_in, cotangent, route_ids, route_gates, norm_gain, up_weight, down_weight):
    section = lax.axis_index("section")
    routes = routing(route_ids, route_gates, section // 2, section % 2)
    dma, vmem = pltpu.SemaphoreType.DMA, pltpu.VMEM
    whole = pl.BlockSpec(memory_space=pltpu.VMEM)
    messages = vmem((6, BATCHES, EXPERTS, MSG, PART), BF16)
    features = vmem((BATCHES, SLOTS, PART), BF16)
    hidden = vmem((4, BATCHES, SLOTS, 2 * HALF), BF16)
    quarters = vmem((BATCHES, QUART, 2 * HALF), F32)
    cut = vmem((BATCHES, GROUPS, BLOCK, PART), BF16)
    up_half, down_half = vmem((PART, HALF), BF16), vmem((HALF, PART), BF16)
    scratch = [
        cut, cut, up_half, down_half,
        vmem((3, 16, TOKENS), F32), vmem((16, TOKENS), F32), vmem((TOKENS, TOKENS), F32),
        messages, messages, features, features, features, features,
        hidden, vmem((4, BATCHES, 3, QUART, 2 * HALF), BF16), hidden, quarters, quarters,
        vmem((3, BATCHES, 8, TOKENS), F32), vmem((3, BATCHES, 3, 8, TOKENS), F32), vmem((BATCHES, TOKENS, 1), F32),
        vmem((2, BATCHES, TOKENS, PART), BF16), vmem((2, BATCHES, 2, TOKENS, PART), BF16),
        vmem((PART, 2 * HALF), F32), vmem((2 * HALF, PART), F32),
        up_half, down_half, up_half, down_half,
        dma((2, 2, BATCHES, 4)), dma((2, 4)), dma((2, 3)), dma((3, BATCHES, 2, 3)), dma((6, BATCHES, 2)),
        dma((4, BATCHES, 2, 3)), dma((4, BATCHES, 2, 6)), dma((2, BATCHES, 2, 2)),
    ]
    grad_up, grad_down = pl.pallas_call(
        update,
        out_shape=[jax.ShapeDtypeStruct((PART, HALF), BF16), jax.ShapeDtypeStruct((HALF, PART), BF16)],
        in_specs=[whole] * 6,
        out_specs=[whole] * 2,
        scratch_shapes=scratch,
        compiler_params=pltpu.CompilerParams(
            collective_id=0, has_side_effects=True, vmem_limit_bytes=VMEM_LIMIT
        ),
    )(stream_in, cotangent, up_weight[0, 0], down_weight[0, 0], norm_gain, routes)
    return grad_up[None, None], grad_down[None, None]


def solution(mesh):
    placed = (
        P(None, None, ("expert", "dp"), "section"),
        P(None, None, ("expert", "dp"), "section"),
        P(None, None, None, ("expert", "dp"), None),
        P(None, None, None, ("expert", "dp"), None),
        P(),
        P("section", "expert", "dp", None),
        P("section", "expert", None, "dp"),
    )
    return jax.shard_map(
        local,
        mesh=mesh,
        in_specs=placed,
        out_specs=(P("section", "expert", "dp", None), P("section", "expert", None, "dp")),
        check_vma=False,
    )
```

```python
import jax
import jax.numpy as jnp
from jax import lax
from jax.experimental import pallas as pl
from jax.experimental.pallas import tpu as pltpu
from jax.sharding import PartitionSpec as P

EPSILON = 1e-06
MESH = pl.DeviceIdType.MESH
F32 = jnp.float32
BF16 = jnp.bfloat16
EXPERTS = 32
GROUPS = 4
BATCHES = 2
BLOCK = 32
TOKENS = GROUPS * BLOCK
MSG = 8
SLOTS = EXPERTS * MSG
QUART = SLOTS // GROUPS
PART = 896
HALF = 512
VMEM_LIMIT = 56 * 1024 * 1024


def dot(a, b):
    return lax.dot_general(a, b, (((1,), (0,)), ((), ())), preferred_element_type=F32)


def dot_t(a, b):
    return lax.dot_general(a, b, (((1,), (1,)), ((), ())), preferred_element_type=F32)


def t_dot(a, b):
    return lax.dot_general(a, b, (((0,), (0,)), ((), ())), preferred_element_type=F32)


def copy_to(src, dst, send_sem, recv_sem, device):
    return pltpu.make_async_remote_copy(
        src_ref=src,
        dst_ref=dst,
        send_sem=send_sem,
        recv_sem=recv_sem,
        device_id=device,
        device_id_type=MESH,
    )


class Place:
    def __init__(self):
        self.section = lax.axis_index("section")
        self.expert = lax.axis_index("expert")
        self.group = lax.axis_index("dp")
        self.half = self.section % 2
        self.pair = self.section // 2
        self.partner = self.section + 1 - 2 * self.half


def greet_experts(here, barrier):
    def one(k, carry):
        pl.semaphore_signal(
            barrier,
            inc=1,
            device_id={"expert": (here.expert + k) % EXPERTS},
            device_id_type=MESH,
        )
        return carry

    lax.fori_loop(1, EXPERTS, one, 0)


def greet(barrier, device):
    pl.semaphore_signal(barrier, inc=1, device_id=device, device_id_type=MESH)


class Exchange:
    def __init__(self, here, src, dst, sems, sign):
        self.here, self.src, self.dst, self.sems, self.sign = here, src, dst, sems, sign

    def copy(self, k, count=1):
        which = pl.ds(k, count)
        peer = (self.here.expert + self.sign * k + EXPERTS) % EXPERTS
        return copy_to(
            self.src.at[which], self.dst.at[which], self.sems.at[0], self.sems.at[1], {"expert": peer}
        )

    def start(self, rows):
        messages = rows.reshape(EXPERTS, MSG, PART).astype(BF16)
        self.src[...] = messages
        self.dst[0:1] = messages[0:1]

        def one(k, carry):
            self.copy(k).start()
            return carry

        lax.fori_loop(1, EXPERTS, one, 0)

    def take(self):
        self.copy(1, EXPERTS - 1).wait_recv()
        return self.dst[...].astype(F32).reshape(SLOTS, PART).astype(BF16)

    def wait_send(self):
        self.copy(1, EXPERTS - 1).wait_send()


class GroupSum:
    def __init__(self, here, parts, landed, sems):
        self.here, self.parts, self.landed, self.sems = here, parts, landed, sems

    def part(self, away, half):
        quarter = (self.here.group + away) % GROUPS
        rows = pl.ds(pl.multiple_of(quarter * QUART, QUART), QUART)
        return self.parts.at[rows, pl.ds(half * HALF, HALF)]

    def copy(self, slot):
        away, half, to = ((2, 0, 1), (2, 1, 3), (1, 1, 1), (3, 0, 3), (1, 0, 1), (3, 1, 3))[slot]
        return copy_to(
            self.part(away, half), self.landed.at[slot], self.sems.at[0, slot], self.sems.at[1, slot],
            {"dp": (self.here.group + to) % GROUPS},
        )

    def start(self, near, far):
        self.parts[:, 0:HALF] = near.astype(BF16)
        self.parts[:, HALF:] = far.astype(BF16)
        for slot in range(4):
            self.copy(slot).start()

    def pass_on(self):
        for slot, away in ((0, 1), (1, 3)):
            self.copy(slot).wait_recv()
            part = self.part(away, slot)
            part[...] = (part[...].astype(F32) + self.landed[slot].astype(F32)).astype(BF16)
            self.copy(slot + 4).start()

    def total(self):
        for slot in range(2, 6):
            self.copy(slot).wait_recv()

        def half(i, one, other):
            return self.part(0, i)[...].astype(F32) + self.landed[one].astype(F32) + self.landed[other].astype(F32)

        return jnp.concatenate([half(0, 3, 4), half(1, 2, 5)], axis=1)

    def wait_send(self):
        for slot in range(6):
            self.copy(slot).wait_send()


class GroupGather:
    def __init__(self, here, whole, sems):
        self.here, self.whole, self.sems = here, whole, sems

    def rows(self, back):
        quarter = (self.here.group + GROUPS - back) % GROUPS
        return pl.ds(pl.multiple_of(quarter * QUART, QUART), QUART)

    def copy(self, to, back, half, slot):
        where = self.whole.at[self.rows(back), pl.ds(half * HALF, HALF)]
        return copy_to(
            where, where, self.sems.at[0, slot], self.sems.at[1, slot],
            {"dp": (self.here.group + to) % GROUPS},
        )

    def start(self, value):
        self.whole[self.rows(0)] = value
        for slot, (to, half) in enumerate(((1, 0), (3, 1), (1, 1), (3, 0))):
            self.copy(to, 0, half, slot).start()

    def start_near(self, value):
        self.whole[self.rows(0), 0:HALF] = value
        self.copy(1, 0, 0, 0).start()
        self.copy(3, 0, 0, 3).start()

    def start_far(self):
        self.copy(3, 0, 1, 1).start()
        self.copy(1, 0, 1, 2).start()

    def pass_on(self):
        self.copy(1, 1, 0, 0).wait_recv()
        self.copy(1, 1, 0, 4).start()
        self.copy(3, 3, 1, 1).wait_recv()
        self.copy(3, 3, 1, 5).start()

    def wait_recv(self):
        self.copy(1, 1, 1, 2).wait_recv()
        self.copy(3, 3, 0, 3).wait_recv()
        self.copy(1, 2, 0, 4).wait_recv()
        self.copy(3, 2, 1, 5).wait_recv()

    def wait_send(self):
        for slot, (to, half) in enumerate(((1, 0), (3, 1), (1, 1), (3, 0))):
            self.copy(to, 0, half, slot).wait_send()
        self.copy(1, 1, 0, 4).wait_send()
        self.copy(3, 3, 1, 5).wait_send()


class SmallSum:
    def __init__(self, here, own, landed, sems):
        self.here, self.own, self.landed, self.sems = here, own, landed, sems

    def copy(self, j):
        return copy_to(
            self.own,
            self.landed.at[j - 1],
            self.sems.at[0, j - 1],
            self.sems.at[1, j - 1],
            {"dp": (self.here.group + j) % GROUPS},
        )

    def start(self):
        for j in (2, 1, 3):
            self.copy(j).start()

    def start_column(self, column):
        self.own[...] = jnp.broadcast_to(column, (TOKENS, TOKENS)).T[0:8]
        self.start()

    def total(self):
        for j in (1, 3, 2):
            self.copy(j).wait_recv()
        return self.own[...] + self.landed[0] + self.landed[1] + self.landed[2]

    def total_column(self):
        return jnp.broadcast_to(self.total()[0:1], (TOKENS, TOKENS)).T[:, 0:1]

    def wait_send(self):
        for j in (1, 2, 3):
            self.copy(j).wait_send()


class HandOn:
    def __init__(self, here, leaving, handed, sems):
        self.here, self.leaving, self.handed, self.sems = here, leaving, handed, sems

    def copy(self, to, owner):
        return copy_to(
            self.leaving, self.handed.at[owner], self.sems.at[0, to], self.sems.at[1, owner],
            {"section": 2 * (1 - self.here.pair) + to},
        )

    def start(self, value):
        self.leaving[...] = value.astype(BF16)
        for to in range(2):
            self.copy(to, self.here.half).start()

    def take(self):
        for owner in range(2):
            self.copy(0, owner).wait_recv()
        return (self.handed[0].astype(F32) + self.handed[1].astype(F32)).astype(BF16)

    def again(self):
        return (self.handed[0].astype(F32) + self.handed[1].astype(F32)).astype(BF16)

    def wait_send(self):
        for to in range(2):
            self.copy(to, self.here.half).wait_send()


class Cut:
    def __init__(self, here, source, middle, target, sems, flip):
        self.here, self.source, self.middle, self.target = here, source, middle, target
        self.sems, self.flip = sems, flip

    def rows(self, m, section):
        pair = section // 2
        return self.source.at[1 - pair if self.flip else pair, m]

    def across(self, m, j, owner):
        to = (self.here.section + j) % 4
        return copy_to(
            self.rows(m, to), self.middle.at[m, owner],
            self.sems.at[0, 0, m, j - 1], self.sems.at[0, 1, m, j - 1], {"section": to},
        )

    def within(self, m, j, owner):
        to = (self.here.group + j) % GROUPS
        return copy_to(
            self.middle.at[m, to], self.target.at[m, owner],
            self.sems.at[1, 0, m, j - 1], self.sems.at[1, 1, m, j - 1], {"dp": to},
        )

    def start(self, m):
        for j in (2, 1, 3):
            self.across(m, j, self.here.section).start()
        self.middle[m, pl.ds(self.here.section, 1)] = self.rows(m, self.here.section)[...][None]

    def pass_on(self, m):
        for j in (1, 3, 2):
            self.across(m, j, (self.here.section + 4 - j) % 4).wait_recv()
        for j in (2, 1, 3):
            self.within(m, j, self.here.group).start()
        own = pl.ds(self.here.group, 1)
        self.target[m, own] = self.middle[m, own]

    def take(self, m):
        for j in (1, 3, 2):
            self.within(m, j, (self.here.group + GROUPS - j) % GROUPS).wait_recv()

    def value(self, m):
        return self.target[m].reshape(TOKENS, PART)

    def wait_send(self):
        for m in range(BATCHES):
            for j in (1, 2, 3):
                self.across(m, j, self.here.section).wait_send()
                self.within(m, j, self.here.group).wait_send()


class Routes:
    def __init__(self, rows, columns):
        self.rows, self.columns = rows, columns

    def by_slot(self, u, m):
        slots = lax.broadcasted_iota(jnp.int32, (SLOTS, TOKENS), 0).astype(F32)
        at = m * 8 + u * 4
        return [(slots == self.rows[at + 2 * k : at + 2 * k + 1], self.rows[at + 2 * k + 1 : at + 2 * k + 2]) for k in range(2)]

    def by_token(self, u, m):
        slots = lax.broadcasted_iota(jnp.int32, (TOKENS, SLOTS), 1).astype(F32)
        at = m * 8 + u * 4
        return [(slots == self.columns[:, at + 2 * k : at + 2 * k + 1], self.columns[:, at + 2 * k + 1 : at + 2 * k + 2]) for k in range(2)]


def marks(picks):
    (first, _), (second, _) = picks
    return jnp.where(first | second, 1.0, 0.0).astype(BF16)


def weighted(picks):
    (first, share), (second, other) = picks
    return jnp.where(first, share, 0.0) + jnp.where(second, other, 0.0)


def exact_dot(weights, values):
    high = weights.astype(BF16)
    low = (weights - high.astype(F32)).astype(BF16)
    return dot(high, values) + dot(low, values)


def norm_scale(total):
    return lax.rsqrt(total * (1.0 / (GROUPS * PART)) + EPSILON)


def silu(pre):
    return pre * jax.nn.sigmoid(pre)


def pre_gradient(act_grad, pre):
    gate = jax.nn.sigmoid(pre)
    return (act_grad * gate * (1.0 + pre * (1.0 - gate))).astype(BF16)


def row_sum(values):
    return jnp.sum(values, axis=1, keepdims=True)


def update(
    stream, cotangent, up, down, norm_gain, routes_own,
    grad_up, grad_down,
    middle_in, middle_cotan, layer_in, cotan, up_other, down_other, routes_landed, routes_rows, routes_columns,
    sent, came, rows1, rows1_other, rows2, grads1, grads2, parts, landed, gathered, pre1, pre2,
    small_own, small_landed, scales, leaving, handed,
    sum_up, sum_down, give_up, give_down, got_up, got_down, far_quarter,
    cut_sems, pair_sems, far_sems, route_sems, small_sems, peer_sems, sum_sems, gather_sems, hand_sems,
):
    here = Place()
    both = range(BATCHES)
    barrier = pltpu.get_barrier_semaphore()
    greet_experts(here, barrier)

    def greet_other(i, carry):
        at = (here.section * GROUPS + here.group + i) % 16
        greet(barrier, {"section": at // GROUPS, "dp": at % GROUPS})
        return carry

    lax.fori_loop(1, 16, greet_other, 0)
    pl.semaphore_wait(barrier, EXPERTS - 1 + 15)

    def exchanges(i, sign):
        return [Exchange(here, sent.at[i, m], came.at[i, m], peer_sems.at[i, m], sign) for m in both]

    go1, back1, go_grads, go2, back2, go3 = (
        exchanges(i, sign) for i, sign in enumerate((1, -1, 1, 1, -1, 1))
    )
    sum1, sum2, sum_grads2, sum_grads1 = (
        [GroupSum(here, parts.at[i, m], landed.at[i, m], sum_sems.at[i, m]) for m in both] for i in range(4)
    )
    act1, act2, pre_grad2, pre_grad1 = ([gathered.at[i, m] for m in both] for i in range(4))
    all_act1, all_act2, all_pre_grad2, all_pre_grad1 = (
        [GroupGather(here, gathered.at[i, m], gather_sems.at[i, m]) for m in both] for i in range(4)
    )
    norm1, norm2, mix = (
        [SmallSum(here, small_own.at[i, m], small_landed.at[i, m], small_sems.at[i, m]) for m in both]
        for i in range(3)
    )
    hand1, hand2 = (
        [HandOn(here, leaving.at[i, m], handed.at[i, m], hand_sems.at[i, m]) for m in both] for i in range(2)
    )
    cut_in = Cut(here, stream, middle_in, layer_in, cut_sems.at[0], False)
    cut_cotan = Cut(here, cotangent, middle_cotan, cotan, cut_sems.at[1], True)
    route_sum = SmallSum(here, routes_own, routes_landed, route_sems)
    routes = Routes(routes_rows, routes_columns)
    to_partner = {"section": here.partner}

    def pair_copy(i, source, target):
        return copy_to(source, target, pair_sems.at[0, i], pair_sems.at[1, i], to_partner)

    up_copy, down_copy = pair_copy(0, up, up_other), pair_copy(1, down, down_other)
    give_down_copy, give_up_copy = pair_copy(2, give_down, got_down), pair_copy(3, give_up, got_up)
    rows_copy = pair_copy(4, rows1, rows1_other)
    own_quarter = pl.ds(pl.multiple_of(here.group * QUART, QUART), QUART)
    far_copies = [
        copy_to(
            far_quarter.at[m], gathered.at[3, m, own_quarter, pl.ds(HALF, HALF)],
            far_sems.at[0, m], far_sems.at[1, m], to_partner,
        )
        for m in both
    ]
    gain = norm_gain[pl.ds(here.pair, 1), pl.ds(pl.multiple_of(here.group * PART, PART), PART)]
    first_half = (1 - here.half).astype(F32)

    def up_parts(rows, target):
        target.start(dot(rows[...], up[...]), dot(rows[...], up_other[...]))

    def down_parts(rows, target):
        target.start(dot_t(rows[...], down[...]), dot_t(rows[...], down_other[...]))

    route_sum.start()
    for m in both:
        cut_in.start(m)
    for m in both:
        cut_cotan.start(m)
    for m in both:
        cut_in.pass_on(m)
    up_copy.start()
    for m in both:
        cut_in.take(m)
        values = cut_in.value(m).astype(F32)
        norm1[m].start_column(row_sum(values * values))
    total = route_sum.total()
    routes_rows[...] = total
    routes_columns[...] = jnp.concatenate([total] * (TOKENS // total.shape[0]), axis=0).T
    for m in both:
        scale = norm_scale(norm1[m].total_column())
        normed = (cut_in.value(m).astype(F32) * scale * gain).astype(BF16)
        go1[m].start(dot(marks(routes.by_slot(0, m)), normed))
    for m in both:
        cut_cotan.pass_on(m)
    up_copy.wait_recv()
    down_copy.start()
    for m in both:
        rows1[m] = go1[m].take()
        up_parts(rows1.at[m], sum1[m])
    for m in both:
        sum1[m].pass_on()
    for m in both:
        cut_cotan.take(m)
        go_grads[m].start(exact_dot(weighted(routes.by_slot(1, m)), cut_cotan.value(m)))
    for m in both:
        pre1[m] = sum1[m].total()
        all_act1[m].start(silu(pre1[m]).astype(BF16))
    for m in both:
        all_act1[m].pass_on()
    down_copy.wait_recv()
    for m in both:
        all_act1[m].wait_recv()
        act = act1[m]
        back1[m].start(dot(act[:, 0:HALF], down[...]) + dot(act[:, HALF:], down_other[...]))
    for m in both:
        grads2[m] = go_grads[m].take()
        down_parts(grads2.at[m], sum_grads2[m])
    for m in both:
        expert_out = back1[m].take()
        direct = cut_in.value(m).astype(F32) * first_half
        hand1[m].start(direct + exact_dot(weighted(routes.by_token(0, m)), expert_out))
    for m in both:
        sum_grads2[m].pass_on()

    for m in both:
        values = hand1[m].take().astype(F32)
        norm2[m].start_column(row_sum(values * values))
        scales[m] = norm_scale(norm2[m].total_column())
        normed = (hand1[m].again().astype(F32) * scales[m] * gain).astype(BF16)
        go2[m].start(dot(marks(routes.by_slot(1, m)), normed))
    for m in both:
        rows2[m] = go2[m].take()
        up_parts(rows2.at[m], sum2[m])
    rows_copy.start()
    for m in both:
        sum2[m].pass_on()
    for m in both:
        pre2[m] = sum2[m].total()
        all_pre_grad2[m].start(pre_gradient(sum_grads2[m].total(), pre2[m]))
    for m in both:
        all_pre_grad2[m].pass_on()
    for m in both:
        all_pre_grad2[m].wait_recv()
        grad = pre_grad2[m]
        back2[m].start(dot_t(grad[:, 0:HALF], up[...]) + dot_t(grad[:, HALF:], up_other[...]))
    for m in both:
        all_act2[m].start(silu(pre2[m]).astype(BF16))

    @pl.loop(0, PART // 128)
    def _(i):
        at = pl.ds(pl.multiple_of(i * 128, 128), 128)
        value = t_dot(rows2[0, :, at], pre_grad2[0][...]) + t_dot(rows2[1, :, at], pre_grad2[1][...])
        sum_up[at] = value[:, 0:HALF]
        give_up[at] = value[:, HALF:].astype(BF16)

    for m in both:
        scaled = dot(marks(routes.by_token(1, m)), back2[m].take()) * gain
        mix[m].start_column(row_sum(hand1[m].again().astype(F32) * scaled))
        direct = cut_cotan.value(m).astype(F32) * first_half + scales[m] * scaled
        mean = mix[m].total_column() * (1.0 / (GROUPS * PART))
        scale = scales[m]
        hand2[m].start(direct - hand1[m].again().astype(F32) * (scale * scale * scale * mean))
    for m in both:
        all_act2[m].pass_on()
    for m in both:
        all_act2[m].wait_recv()

    @pl.loop(0, 2 * HALF // 128)
    def _(i):
        at = pl.ds(pl.multiple_of(i * 128, 128), 128)
        sum_down[at] = t_dot(act2[0][:, at], grads2[0]) + t_dot(act2[1][:, at], grads2[1])

    for m in both:
        incoming = hand2[m].take()
        go3[m].start(exact_dot(weighted(routes.by_slot(0, m)), incoming))
    give_up_copy.start()
    for m in both:
        grads1[m] = go3[m].take()
        down_parts(grads1.at[m], sum_grads1[m])
    for m in both:
        sum_grads1[m].pass_on()

    @pl.loop(0, HALF // 128)
    def _(i):
        at = pl.ds(pl.multiple_of(i * 128, 128), 128)
        far = pl.ds(pl.multiple_of(HALF + i * 128, 128), 128)
        value = sum_down[far] + t_dot(act1[0][:, far], grads1[0]) + t_dot(act1[1][:, far], grads1[1])
        give_down[at] = value.astype(BF16)

    give_down_copy.start()
    for m in both:
        quarter = pre_gradient(sum_grads1[m].total(), pre1[m])
        far_quarter[m] = quarter[:, HALF:]
        far_copies[m].start()
        all_pre_grad1[m].start_near(quarter[:, 0:HALF])
    for m in both:
        far_copies[m].wait_recv()
        all_pre_grad1[m].start_far()
    for m in both:
        all_pre_grad1[m].pass_on()

    @pl.loop(0, HALF // 128)
    def _(i):
        at = pl.ds(pl.multiple_of(i * 128, 128), 128)
        sum_down[at] += t_dot(act1[0][:, at], grads1[0]) + t_dot(act1[1][:, at], grads1[1])

    give_up_copy.wait_recv()
    sum_up[...] += got_up[...].astype(F32)
    rows_copy.wait_recv()
    for m in both:
        all_pre_grad1[m].wait_recv()

    @pl.loop(0, PART // 128)
    def _(i):
        at = pl.ds(pl.multiple_of(i * 128, 128), 128)
        value = sum_up[at]
        for m in both:
            value = value + t_dot(rows1[m, :, at], pre_grad1[m][:, 0:HALF])
            value = value + t_dot(rows1_other[m, :, at], pre_grad1[m][:, HALF:])
        grad_up[at] = value.astype(BF16)

    give_down_copy.wait_recv()
    grad_down[...] = (sum_down[0:HALF] + got_down[...].astype(F32)).astype(BF16)

    for sender in (cut_in, cut_cotan, route_sum, up_copy, down_copy, give_down_copy, give_up_copy, rows_copy, *far_copies):
        sender.wait_send()
    for senders in (go1, back1, go_grads, go2, back2, go3, sum1, sum2, sum_grads2, sum_grads1, all_act1,
                    all_act2, all_pre_grad2, all_pre_grad1, norm1, norm2, mix, hand1, hand2):
        for m in both:
            senders[m].wait_send()


def routing(route_ids, route_gates, pair, half):
    ids = lax.dynamic_index_in_dim(route_ids, pair, 0, keepdims=False)
    gates = lax.dynamic_index_in_dim(route_gates, pair, 0, keepdims=False)
    shares = gates / jnp.sum(gates, axis=-1, keepdims=True)
    ids, shares = (jnp.where(pair == 0, value, value[::-1]) for value in (ids, shares))
    uses, batches, tokens, top = ids.shape
    flat = ids.reshape(uses, batches, tokens * top)
    before = jnp.tri(tokens * top, k=-1, dtype=jnp.bool_)
    position = jnp.sum((flat[..., :, None] == flat[..., None, :]) & before, axis=-1)
    away = (flat - lax.axis_index("expert") + EXPERTS) % EXPERTS
    group = lax.axis_index("dp")
    slot = away * MSG + group * 2 + position % 2
    slot = jnp.where(position // 2 == half, slot, -1).astype(F32).reshape(ids.shape)
    values = jnp.stack([slot, shares], axis=-1).transpose(1, 0, 3, 4, 2).reshape(batches * uses * top * 2, tokens)
    lanes = jnp.arange(TOKENS, dtype=jnp.int32)[None, :] // BLOCK
    return jnp.where(lanes == group, jnp.tile(values, (1, GROUPS)), 0.0)


def local(stream_in, cotangent, route_ids, route_gates, norm_gain, up_weight, down_weight):
    section = lax.axis_index("section")
    routes = routing(route_ids, route_gates, section // 2, section % 2)
    dma, vmem = pltpu.SemaphoreType.DMA, pltpu.VMEM
    whole = pl.BlockSpec(memory_space=pltpu.VMEM)
    messages = vmem((6, BATCHES, EXPERTS, MSG, PART), BF16)
    features = vmem((BATCHES, SLOTS, PART), BF16)
    hidden = vmem((4, BATCHES, SLOTS, 2 * HALF), BF16)
    quarters = vmem((BATCHES, QUART, 2 * HALF), F32)
    cut = vmem((BATCHES, GROUPS, BLOCK, PART), BF16)
    up_half, down_half = vmem((PART, HALF), BF16), vmem((HALF, PART), BF16)
    scratch = [
        cut, cut, cut, cut, up_half, down_half,
        vmem((3, 16, TOKENS), F32), vmem((16, TOKENS), F32), vmem((TOKENS, TOKENS), F32),
        messages, messages, features, features, features, features, features,
        hidden, vmem((4, BATCHES, 6, QUART, HALF), BF16), hidden, quarters, quarters,
        vmem((3, BATCHES, 8, TOKENS), F32), vmem((3, BATCHES, 3, 8, TOKENS), F32), vmem((BATCHES, TOKENS, 1), F32),
        vmem((2, BATCHES, TOKENS, PART), BF16), vmem((2, BATCHES, 2, TOKENS, PART), BF16),
        vmem((PART, HALF), F32), vmem((2 * HALF, PART), F32),
        up_half, down_half, up_half, down_half, vmem((BATCHES, QUART, HALF), BF16),
        dma((2, 2, 2, BATCHES, 3)), dma((2, 5)), dma((2, BATCHES)), dma((2, 3)), dma((3, BATCHES, 2, 3)), dma((6, BATCHES, 2)),
        dma((4, BATCHES, 2, 6)), dma((4, BATCHES, 2, 6)), dma((2, BATCHES, 2, 2)),
    ]
    grad_up, grad_down = pl.pallas_call(
        update,
        out_shape=[jax.ShapeDtypeStruct((PART, HALF), BF16), jax.ShapeDtypeStruct((HALF, PART), BF16)],
        in_specs=[whole] * 6,
        out_specs=[whole] * 2,
        scratch_shapes=scratch,
        compiler_params=pltpu.CompilerParams(
            collective_id=0, has_side_effects=True, vmem_limit_bytes=VMEM_LIMIT
        ),
    )(stream_in, cotangent, up_weight[0, 0], down_weight[0, 0], norm_gain, routes)
    return grad_up[None, None], grad_down[None, None]


def solution(mesh):
    placed = (
        P(None, None, ("expert", "dp"), "section"),
        P(None, None, ("expert", "dp"), "section"),
        P(None, None, None, ("expert", "dp"), None),
        P(None, None, None, ("expert", "dp"), None),
        P(),
        P("section", "expert", "dp", None),
        P("section", "expert", None, "dp"),
    )
    return jax.shard_map(
        local,
        mesh=mesh,
        in_specs=placed,
        out_specs=(P("section", "expert", "dp", None), P("section", "expert", None, "dp")),
        check_vma=False,
    )
```

```python
import jax
import jax.numpy as jnp
from jax import lax
from jax.experimental import pallas as pl
from jax.experimental.pallas import tpu as pltpu
from jax.sharding import PartitionSpec as P

EPSILON = 1e-06
MESH = pl.DeviceIdType.MESH
F32 = jnp.float32
BF16 = jnp.bfloat16
EXPERTS = 32
GROUPS = 4
BATCHES = 2
BLOCK = 32
TOKENS = GROUPS * BLOCK
MSG = 8
SLOTS = EXPERTS * MSG
QUART = SLOTS // GROUPS
PART = 896
HALF = 512
VMEM_LIMIT = 56 * 1024 * 1024


def dot(a, b):
    return lax.dot_general(a, b, (((1,), (0,)), ((), ())), preferred_element_type=F32)


def dot_t(a, b):
    return lax.dot_general(a, b, (((1,), (1,)), ((), ())), preferred_element_type=F32)


def t_dot(a, b):
    return lax.dot_general(a, b, (((0,), (0,)), ((), ())), preferred_element_type=F32)


def copy_to(src, dst, send_sem, recv_sem, device):
    return pltpu.make_async_remote_copy(
        src_ref=src,
        dst_ref=dst,
        send_sem=send_sem,
        recv_sem=recv_sem,
        device_id=device,
        device_id_type=MESH,
    )


class Place:
    def __init__(self):
        self.section = lax.axis_index("section")
        self.expert = lax.axis_index("expert")
        self.group = lax.axis_index("dp")
        self.half = self.section % 2
        self.pair = self.section // 2
        self.partner = self.section + 1 - 2 * self.half


def greet_experts(here, barrier):
    def one(k, carry):
        pl.semaphore_signal(
            barrier,
            inc=1,
            device_id={"expert": (here.expert + k) % EXPERTS},
            device_id_type=MESH,
        )
        return carry

    lax.fori_loop(1, EXPERTS, one, 0)


def greet(barrier, device):
    pl.semaphore_signal(barrier, inc=1, device_id=device, device_id_type=MESH)


class Exchange:
    def __init__(self, here, src, dst, sems, sign):
        self.here, self.src, self.dst, self.sems, self.sign = here, src, dst, sems, sign

    def copy(self, k, count=1):
        which = pl.ds(k, count)
        peer = (self.here.expert + self.sign * k + EXPERTS) % EXPERTS
        return copy_to(
            self.src.at[which], self.dst.at[which], self.sems.at[0], self.sems.at[1], {"expert": peer}
        )

    def start(self, rows):
        messages = rows.reshape(EXPERTS, MSG, PART).astype(BF16)
        self.src[...] = messages
        self.dst[0:1] = messages[0:1]

        def one(k, carry):
            self.copy(k).start()
            return carry

        lax.fori_loop(1, EXPERTS, one, 0)

    def take(self):
        self.copy(1, EXPERTS - 1).wait_recv()
        return self.dst[...].astype(F32).reshape(SLOTS, PART).astype(BF16)

    def wait_send(self):
        self.copy(1, EXPERTS - 1).wait_send()


class GroupSum:
    def __init__(self, here, parts, landed, sems):
        self.here, self.parts, self.landed, self.sems = here, parts, landed, sems

    def part(self, away, half):
        quarter = (self.here.group + away) % GROUPS
        rows = pl.ds(pl.multiple_of(quarter * QUART, QUART), QUART)
        return self.parts.at[rows, pl.ds(half * HALF, HALF)]

    def copy(self, slot):
        away, half, to = ((2, 0, 1), (2, 1, 3), (1, 1, 1), (3, 0, 3), (1, 0, 1), (3, 1, 3))[slot]
        return copy_to(
            self.part(away, half), self.landed.at[slot], self.sems.at[0, slot], self.sems.at[1, slot],
            {"dp": (self.here.group + to) % GROUPS},
        )

    def start(self, near, far):
        self.parts[:, 0:HALF] = near.astype(BF16)
        self.parts[:, HALF:] = far.astype(BF16)
        for slot in range(4):
            self.copy(slot).start()

    def pass_on(self):
        for slot, away in ((0, 1), (1, 3)):
            self.copy(slot).wait_recv()
            part = self.part(away, slot)
            part[...] = (part[...].astype(F32) + self.landed[slot].astype(F32)).astype(BF16)
            self.copy(slot + 4).start()

    def total(self):
        for slot in range(2, 6):
            self.copy(slot).wait_recv()

        def half(i, one, other):
            return self.part(0, i)[...].astype(F32) + self.landed[one].astype(F32) + self.landed[other].astype(F32)

        return jnp.concatenate([half(0, 3, 4), half(1, 2, 5)], axis=1)

    def wait_send(self):
        for slot in range(6):
            self.copy(slot).wait_send()


class GroupGather:
    def __init__(self, here, whole, sems):
        self.here, self.whole, self.sems = here, whole, sems

    def rows(self, back):
        quarter = (self.here.group + GROUPS - back) % GROUPS
        return pl.ds(pl.multiple_of(quarter * QUART, QUART), QUART)

    def copy(self, to, back, half, slot):
        where = self.whole.at[self.rows(back), pl.ds(half * HALF, HALF)]
        return copy_to(
            where, where, self.sems.at[0, slot], self.sems.at[1, slot],
            {"dp": (self.here.group + to) % GROUPS},
        )

    def start(self, value):
        self.whole[self.rows(0)] = value
        for slot, (to, half) in enumerate(((1, 0), (3, 1), (1, 1), (3, 0))):
            self.copy(to, 0, half, slot).start()

    def start_near(self, value):
        self.whole[self.rows(0), 0:HALF] = value
        self.copy(1, 0, 0, 0).start()
        self.copy(3, 0, 0, 3).start()

    def start_far(self):
        self.copy(3, 0, 1, 1).start()
        self.copy(1, 0, 1, 2).start()

    def pass_on(self):
        self.copy(1, 1, 0, 0).wait_recv()
        self.copy(1, 1, 0, 4).start()
        self.copy(3, 3, 1, 1).wait_recv()
        self.copy(3, 3, 1, 5).start()

    def wait_recv(self):
        self.copy(1, 1, 1, 2).wait_recv()
        self.copy(3, 3, 0, 3).wait_recv()
        self.copy(1, 2, 0, 4).wait_recv()
        self.copy(3, 2, 1, 5).wait_recv()

    def wait_send(self):
        for slot, (to, half) in enumerate(((1, 0), (3, 1), (1, 1), (3, 0))):
            self.copy(to, 0, half, slot).wait_send()
        self.copy(1, 1, 0, 4).wait_send()
        self.copy(3, 3, 1, 5).wait_send()


class SmallSum:
    def __init__(self, here, own, landed, sems):
        self.here, self.own, self.landed, self.sems = here, own, landed, sems

    def copy(self, j):
        return copy_to(
            self.own,
            self.landed.at[j - 1],
            self.sems.at[0, j - 1],
            self.sems.at[1, j - 1],
            {"dp": (self.here.group + j) % GROUPS},
        )

    def start(self):
        for j in (2, 1, 3):
            self.copy(j).start()

    def start_column(self, column):
        self.own[...] = jnp.broadcast_to(column, (TOKENS, TOKENS)).T[0:8]
        self.start()

    def total(self):
        for j in (1, 3, 2):
            self.copy(j).wait_recv()
        return self.own[...] + self.landed[0] + self.landed[1] + self.landed[2]

    def total_column(self):
        return jnp.broadcast_to(self.total()[0:1], (TOKENS, TOKENS)).T[:, 0:1]

    def wait_send(self):
        for j in (1, 2, 3):
            self.copy(j).wait_send()


class HandOn:
    def __init__(self, here, leaving, handed, sems):
        self.here, self.leaving, self.handed, self.sems = here, leaving, handed, sems

    def copy(self, to, owner):
        return copy_to(
            self.leaving, self.handed.at[owner], self.sems.at[0, to], self.sems.at[1, owner],
            {"section": 2 * (1 - self.here.pair) + to},
        )

    def start(self, value):
        self.leaving[...] = value.astype(BF16)
        for to in range(2):
            self.copy(to, self.here.half).start()

    def take(self):
        for owner in range(2):
            self.copy(0, owner).wait_recv()
        return (self.handed[0].astype(F32) + self.handed[1].astype(F32)).astype(BF16)

    def again(self):
        return (self.handed[0].astype(F32) + self.handed[1].astype(F32)).astype(BF16)

    def wait_send(self):
        for to in range(2):
            self.copy(to, self.here.half).wait_send()


class Cut:
    def __init__(self, here, source, middle, target, sems, flip):
        self.here, self.source, self.middle, self.target = here, source, middle, target
        self.sems, self.flip = sems, flip

    def rows(self, m, section):
        pair = section // 2
        return self.source.at[1 - pair if self.flip else pair, m]

    def across(self, m, j, owner):
        to = (self.here.section + j) % 4
        return copy_to(
            self.rows(m, to), self.middle.at[m, owner],
            self.sems.at[0, 0, m, j - 1], self.sems.at[0, 1, m, j - 1], {"section": to},
        )

    def within(self, m, j, owner):
        to = (self.here.group + j) % GROUPS
        return copy_to(
            self.middle.at[m, to], self.target.at[m, owner],
            self.sems.at[1, 0, m, j - 1], self.sems.at[1, 1, m, j - 1], {"dp": to},
        )

    def start(self, m):
        for j in (2, 1, 3):
            self.across(m, j, self.here.section).start()
        self.middle[m, pl.ds(self.here.section, 1)] = self.rows(m, self.here.section)[...][None]

    def pass_on(self, m):
        for j in (1, 3, 2):
            self.across(m, j, (self.here.section + 4 - j) % 4).wait_recv()
        for j in (2, 1, 3):
            self.within(m, j, self.here.group).start()
        own = pl.ds(self.here.group, 1)
        self.target[m, own] = self.middle[m, own]

    def take(self, m):
        for j in (1, 3, 2):
            self.within(m, j, (self.here.group + GROUPS - j) % GROUPS).wait_recv()

    def value(self, m):
        return self.target[m].reshape(TOKENS, PART)

    def wait_send(self):
        for m in range(BATCHES):
            for j in (1, 2, 3):
                self.across(m, j, self.here.section).wait_send()
                self.within(m, j, self.here.group).wait_send()


class Routes:
    def __init__(self, rows, columns):
        self.rows, self.columns = rows, columns

    def by_slot(self, u, m):
        slots = lax.broadcasted_iota(jnp.int32, (SLOTS, TOKENS), 0).astype(F32)
        at = m * 8 + u * 4
        return [(slots == self.rows[at + 2 * k : at + 2 * k + 1], self.rows[at + 2 * k + 1 : at + 2 * k + 2]) for k in range(2)]

    def by_token(self, u, m):
        slots = lax.broadcasted_iota(jnp.int32, (TOKENS, SLOTS), 1).astype(F32)
        at = m * 8 + u * 4
        return [(slots == self.columns[:, at + 2 * k : at + 2 * k + 1], self.columns[:, at + 2 * k + 1 : at + 2 * k + 2]) for k in range(2)]


def marks(picks):
    (first, _), (second, _) = picks
    return jnp.where(first | second, 1.0, 0.0).astype(BF16)


def weighted(picks):
    (first, share), (second, other) = picks
    return jnp.where(first, share, 0.0) + jnp.where(second, other, 0.0)


def exact_dot(weights, values):
    high = weights.astype(BF16)
    low = (weights - high.astype(F32)).astype(BF16)
    return dot(high, values) + dot(low, values)


def norm_scale(total):
    return lax.rsqrt(total * (1.0 / (GROUPS * PART)) + EPSILON)


def silu(pre):
    return pre * jax.nn.sigmoid(pre)


def pre_gradient(act_grad, pre):
    gate = jax.nn.sigmoid(pre)
    return (act_grad * gate * (1.0 + pre * (1.0 - gate))).astype(BF16)


def row_sum(values):
    return jnp.sum(values, axis=1, keepdims=True)


def update(
    stream, cotangent, up, down, norm_gain, routes_own,
    grad_up, grad_down,
    middle_in, middle_cotan, layer_in, cotan, up_other, down_other, routes_landed, routes_rows, routes_columns,
    sent, came, rows1, rows1_other, rows2, grads1, grads2, parts, landed, gathered, pre1, pre2,
    small_own, small_landed, scales, leaving, handed,
    sum_up, sum_down, give_up, give_down, got_up, got_down, far_quarter,
    cut_sems, pair_sems, far_sems, route_sems, small_sems, peer_sems, sum_sems, gather_sems, hand_sems,
):
    here = Place()
    both = range(BATCHES)
    barrier = pltpu.get_barrier_semaphore()
    greet_experts(here, barrier)

    def greet_other(i, carry):
        at = (here.section * GROUPS + here.group + i) % 16
        greet(barrier, {"section": at // GROUPS, "dp": at % GROUPS})
        return carry

    lax.fori_loop(1, 16, greet_other, 0)
    pl.semaphore_wait(barrier, EXPERTS - 1 + 15)

    def exchanges(i, sign):
        return [Exchange(here, sent.at[i, m], came.at[i, m], peer_sems.at[i, m], sign) for m in both]

    go1, back1, go_grads, go2, back2, go3 = (
        exchanges(i, sign) for i, sign in enumerate((1, -1, 1, 1, -1, 1))
    )
    sum1, sum2, sum_grads2, sum_grads1 = (
        [GroupSum(here, parts.at[i, m], landed.at[i, m], sum_sems.at[i, m]) for m in both] for i in range(4)
    )
    act1, act2, pre_grad2, pre_grad1 = ([gathered.at[i, m] for m in both] for i in range(4))
    all_act1, all_act2, all_pre_grad2, all_pre_grad1 = (
        [GroupGather(here, gathered.at[i, m], gather_sems.at[i, m]) for m in both] for i in range(4)
    )
    norm1, norm2, mix = (
        [SmallSum(here, small_own.at[i, m], small_landed.at[i, m], small_sems.at[i, m]) for m in both]
        for i in range(3)
    )
    hand1, hand2 = (
        [HandOn(here, leaving.at[i, m], handed.at[i, m], hand_sems.at[i, m]) for m in both] for i in range(2)
    )
    cut_in = Cut(here, stream, middle_in, layer_in, cut_sems.at[0], False)
    cut_cotan = Cut(here, cotangent, middle_cotan, cotan, cut_sems.at[1], True)
    route_sum = SmallSum(here, routes_own, routes_landed, route_sems)
    routes = Routes(routes_rows, routes_columns)
    to_partner = {"section": here.partner}

    def pair_copy(i, source, target):
        return copy_to(source, target, pair_sems.at[0, i], pair_sems.at[1, i], to_partner)

    up_copy, down_copy = pair_copy(0, up, up_other), pair_copy(1, down, down_other)
    give_down_copy, give_up_copy = pair_copy(2, give_down, got_down), pair_copy(3, give_up, got_up)
    rows_copy = pair_copy(4, rows1, rows1_other)
    own_quarter = pl.ds(pl.multiple_of(here.group * QUART, QUART), QUART)
    far_copies = [
        copy_to(
            far_quarter.at[m], gathered.at[3, m, own_quarter, pl.ds(HALF, HALF)],
            far_sems.at[0, m], far_sems.at[1, m], to_partner,
        )
        for m in both
    ]
    gain = norm_gain[pl.ds(here.pair, 1), pl.ds(pl.multiple_of(here.group * PART, PART), PART)]
    first_half = (1 - here.half).astype(F32)

    def up_parts(rows, target):
        target.start(dot(rows[...], up[...]), dot(rows[...], up_other[...]))

    def down_parts(rows, target):
        target.start(dot_t(rows[...], down[...]), dot_t(rows[...], down_other[...]))

    route_sum.start()
    for m in both:
        cut_in.start(m)
    for m in both:
        cut_cotan.start(m)
    for m in both:
        cut_in.pass_on(m)
    up_copy.start()
    for m in both:
        cut_in.take(m)
        values = cut_in.value(m).astype(F32)
        norm1[m].start_column(row_sum(values * values))
    total = route_sum.total()
    routes_rows[...] = total
    routes_columns[...] = jnp.concatenate([total] * (TOKENS // total.shape[0]), axis=0).T
    for m in both:
        scale = norm_scale(norm1[m].total_column())
        normed = (cut_in.value(m).astype(F32) * scale * gain).astype(BF16)
        go1[m].start(dot(marks(routes.by_slot(0, m)), normed))
    for m in both:
        cut_cotan.pass_on(m)
    up_copy.wait_recv()
    down_copy.start()

    def take_rows1(m):
        rows1[m] = go1[m].take()
        up_parts(rows1.at[m], sum1[m])

    def start_grads2(m):
        cut_cotan.take(m)
        go_grads[m].start(exact_dot(weighted(routes.by_slot(1, m)), cut_cotan.value(m)))

    def take_grads2(m):
        grads2[m] = go_grads[m].take()
        down_parts(grads2.at[m], sum_grads2[m])

    def activate1(m):
        pre1[m] = sum1[m].total()
        all_act1[m].start(silu(pre1[m]).astype(BF16))

    def expert_out1(m):
        all_act1[m].wait_recv()
        act = act1[m]
        back1[m].start(dot(act[:, 0:HALF], down[...]) + dot(act[:, HALF:], down_other[...]))

    def leave1(m):
        expert_out = back1[m].take()
        direct = cut_in.value(m).astype(F32) * first_half
        hand1[m].start(direct + exact_dot(weighted(routes.by_token(0, m)), expert_out))

    take_rows1(0)
    sum1[0].pass_on()
    start_grads2(0)
    take_rows1(1)
    activate1(0)
    sum1[1].pass_on()
    all_act1[0].pass_on()
    down_copy.wait_recv()
    expert_out1(0)
    activate1(1)
    all_act1[1].pass_on()
    expert_out1(1)
    take_grads2(0)
    leave1(0)
    sum_grads2[0].pass_on()
    leave1(1)
    start_grads2(1)

    def arrive2(m):
        values = hand1[m].take().astype(F32)
        norm2[m].start_column(row_sum(values * values))
        scales[m] = norm_scale(norm2[m].total_column())
        normed = (hand1[m].again().astype(F32) * scales[m] * gain).astype(BF16)
        go2[m].start(dot(marks(routes.by_slot(1, m)), normed))

    def take_rows2(m):
        rows2[m] = go2[m].take()
        up_parts(rows2.at[m], sum2[m])

    def activate2(m):
        pre2[m] = sum2[m].total()
        all_pre_grad2[m].start(pre_gradient(sum_grads2[m].total(), pre2[m]))

    def row_grads2(m):
        all_pre_grad2[m].wait_recv()
        grad = pre_grad2[m]
        back2[m].start(dot_t(grad[:, 0:HALF], up[...]) + dot_t(grad[:, HALF:], up_other[...]))

    arrive2(0)
    arrive2(1)
    take_grads2(1)
    rows_copy.start()
    take_rows2(0)
    sum_grads2[1].pass_on()
    sum2[0].pass_on()
    take_rows2(1)
    activate2(0)
    sum2[1].pass_on()
    all_pre_grad2[0].pass_on()
    row_grads2(0)
    activate2(1)
    all_pre_grad2[1].pass_on()
    row_grads2(1)
    def collect2(m):
        scaled = dot(marks(routes.by_token(1, m)), back2[m].take()) * gain
        mix[m].start_column(row_sum(hand1[m].again().astype(F32) * scaled))
        return scaled

    def leave2(m, scaled):
        direct = cut_cotan.value(m).astype(F32) * first_half + scales[m] * scaled
        mean = mix[m].total_column() * (1.0 / (GROUPS * PART))
        scale = scales[m]
        hand2[m].start(direct - hand1[m].again().astype(F32) * (scale * scale * scale * mean))

    scaled = collect2(0)
    for m in both:
        all_act2[m].start(silu(pre2[m]).astype(BF16))
    leave2(0, scaled)

    @pl.loop(0, PART // 128)
    def _(i):
        at = pl.ds(pl.multiple_of(i * 128, 128), 128)
        value = t_dot(rows2[0, :, at], pre_grad2[0][...]) + t_dot(rows2[1, :, at], pre_grad2[1][...])
        sum_up[at] = value[:, 0:HALF]
        give_up[at] = value[:, HALF:].astype(BF16)

    scaled = collect2(1)
    for m in both:
        all_act2[m].pass_on()
    leave2(1, scaled)
    for m in both:
        all_act2[m].wait_recv()

    def arrive1(m):
        go3[m].start(exact_dot(weighted(routes.by_slot(0, m)), hand2[m].take()))

    arrive1(0)

    @pl.loop(0, 2 * HALF // 128)
    def _(i):
        at = pl.ds(pl.multiple_of(i * 128, 128), 128)
        sum_down[at] = t_dot(act2[0][:, at], grads2[0]) + t_dot(act2[1][:, at], grads2[1])

    arrive1(1)
    give_up_copy.start()
    def take_grads1(m):
        grads1[m] = go3[m].take()
        down_parts(grads1.at[m], sum_grads1[m])

    def pre_grads1(m):
        quarter = pre_gradient(sum_grads1[m].total(), pre1[m])
        far_quarter[m] = quarter[:, HALF:]
        far_copies[m].start()
        all_pre_grad1[m].start_near(quarter[:, 0:HALF])

    def far_pre_grads1(m):
        far_copies[m].wait_recv()
        all_pre_grad1[m].start_far()

    take_grads1(0)
    sum_grads1[0].pass_on()
    take_grads1(1)
    pre_grads1(0)
    sum_grads1[1].pass_on()
    far_pre_grads1(0)

    @pl.loop(0, HALF // 128)
    def _(i):
        at = pl.ds(pl.multiple_of(i * 128, 128), 128)
        far = pl.ds(pl.multiple_of(HALF + i * 128, 128), 128)
        value = sum_down[far] + t_dot(act1[0][:, far], grads1[0]) + t_dot(act1[1][:, far], grads1[1])
        give_down[at] = value.astype(BF16)

    pre_grads1(1)
    give_down_copy.start()
    all_pre_grad1[0].pass_on()
    far_pre_grads1(1)
    all_pre_grad1[1].pass_on()

    @pl.loop(0, HALF // 128)
    def _(i):
        at = pl.ds(pl.multiple_of(i * 128, 128), 128)
        sum_down[at] += t_dot(act1[0][:, at], grads1[0]) + t_dot(act1[1][:, at], grads1[1])

    give_up_copy.wait_recv()
    sum_up[...] += got_up[...].astype(F32)
    rows_copy.wait_recv()
    for m in both:
        all_pre_grad1[m].wait_recv()

    @pl.loop(0, PART // 128)
    def _(i):
        at = pl.ds(pl.multiple_of(i * 128, 128), 128)
        value = sum_up[at]
        for m in both:
            value = value + t_dot(rows1[m, :, at], pre_grad1[m][:, 0:HALF])
            value = value + t_dot(rows1_other[m, :, at], pre_grad1[m][:, HALF:])
        grad_up[at] = value.astype(BF16)

    give_down_copy.wait_recv()
    grad_down[...] = (sum_down[0:HALF] + got_down[...].astype(F32)).astype(BF16)

    for sender in (cut_in, cut_cotan, route_sum, up_copy, down_copy, give_down_copy, give_up_copy, rows_copy, *far_copies):
        sender.wait_send()
    for senders in (go1, back1, go_grads, go2, back2, go3, sum1, sum2, sum_grads2, sum_grads1, all_act1,
                    all_act2, all_pre_grad2, all_pre_grad1, norm1, norm2, mix, hand1, hand2):
        for m in both:
            senders[m].wait_send()


def routing(route_ids, route_gates, pair, half):
    ids = lax.dynamic_index_in_dim(route_ids, pair, 0, keepdims=False)
    gates = lax.dynamic_index_in_dim(route_gates, pair, 0, keepdims=False)
    shares = gates / jnp.sum(gates, axis=-1, keepdims=True)
    ids, shares = (jnp.where(pair == 0, value, value[::-1]) for value in (ids, shares))
    uses, batches, tokens, top = ids.shape
    flat = ids.reshape(uses, batches, tokens * top)
    before = jnp.tri(tokens * top, k=-1, dtype=jnp.bool_)
    position = jnp.sum((flat[..., :, None] == flat[..., None, :]) & before, axis=-1)
    away = (flat - lax.axis_index("expert") + EXPERTS) % EXPERTS
    group = lax.axis_index("dp")
    slot = away * MSG + group * 2 + position % 2
    slot = jnp.where(position // 2 == half, slot, -1).astype(F32).reshape(ids.shape)
    values = jnp.stack([slot, shares], axis=-1).transpose(1, 0, 3, 4, 2).reshape(batches * uses * top * 2, tokens)
    lanes = jnp.arange(TOKENS, dtype=jnp.int32)[None, :] // BLOCK
    return jnp.where(lanes == group, jnp.tile(values, (1, GROUPS)), 0.0)


def local(stream_in, cotangent, route_ids, route_gates, norm_gain, up_weight, down_weight):
    section = lax.axis_index("section")
    routes = routing(route_ids, route_gates, section // 2, section % 2)
    dma, vmem = pltpu.SemaphoreType.DMA, pltpu.VMEM
    whole = pl.BlockSpec(memory_space=pltpu.VMEM)
    messages = vmem((6, BATCHES, EXPERTS, MSG, PART), BF16)
    features = vmem((BATCHES, SLOTS, PART), BF16)
    hidden = vmem((4, BATCHES, SLOTS, 2 * HALF), BF16)
    quarters = vmem((BATCHES, QUART, 2 * HALF), F32)
    cut = vmem((BATCHES, GROUPS, BLOCK, PART), BF16)
    up_half, down_half = vmem((PART, HALF), BF16), vmem((HALF, PART), BF16)
    scratch = [
        cut, cut, cut, cut, up_half, down_half,
        vmem((3, 16, TOKENS), F32), vmem((16, TOKENS), F32), vmem((TOKENS, TOKENS), F32),
        messages, messages, features, features, features, features, features,
        hidden, vmem((4, BATCHES, 6, QUART, HALF), BF16), hidden, quarters, quarters,
        vmem((3, BATCHES, 8, TOKENS), F32), vmem((3, BATCHES, 3, 8, TOKENS), F32), vmem((BATCHES, TOKENS, 1), F32),
        vmem((2, BATCHES, TOKENS, PART), BF16), vmem((2, BATCHES, 2, TOKENS, PART), BF16),
        vmem((PART, HALF), F32), vmem((2 * HALF, PART), F32),
        up_half, down_half, up_half, down_half, vmem((BATCHES, QUART, HALF), BF16),
        dma((2, 2, 2, BATCHES, 3)), dma((2, 5)), dma((2, BATCHES)), dma((2, 3)), dma((3, BATCHES, 2, 3)), dma((6, BATCHES, 2)),
        dma((4, BATCHES, 2, 6)), dma((4, BATCHES, 2, 6)), dma((2, BATCHES, 2, 2)),
    ]
    grad_up, grad_down = pl.pallas_call(
        update,
        out_shape=[jax.ShapeDtypeStruct((PART, HALF), BF16), jax.ShapeDtypeStruct((HALF, PART), BF16)],
        in_specs=[whole] * 6,
        out_specs=[whole] * 2,
        scratch_shapes=scratch,
        compiler_params=pltpu.CompilerParams(
            collective_id=0, has_side_effects=True, vmem_limit_bytes=VMEM_LIMIT
        ),
    )(stream_in, cotangent, up_weight[0, 0], down_weight[0, 0], norm_gain, routes)
    return grad_up[None, None], grad_down[None, None]


def solution(mesh):
    placed = (
        P(None, None, ("expert", "dp"), "section"),
        P(None, None, ("expert", "dp"), "section"),
        P(None, None, None, ("expert", "dp"), None),
        P(None, None, None, ("expert", "dp"), None),
        P(),
        P("section", "expert", "dp", None),
        P("section", "expert", None, "dp"),
    )
    return jax.shard_map(
        local,
        mesh=mesh,
        in_specs=placed,
        out_specs=(P("section", "expert", "dp", None), P("section", "expert", None, "dp")),
        check_vma=False,
    )
```

```python
import jax
import jax.numpy as jnp
from jax import lax
from jax.experimental import pallas as pl
from jax.experimental.pallas import tpu as pltpu
from jax.sharding import PartitionSpec as P

EPSILON = 1e-06
MESH = pl.DeviceIdType.MESH
F32 = jnp.float32
BF16 = jnp.bfloat16
EXPERTS = 32
GROUPS = 4
BATCHES = 2
BLOCK = 32
TOKENS = GROUPS * BLOCK
MSG = 8
SLOTS = EXPERTS * MSG
QUART = SLOTS // GROUPS
PART = 896
HALF = 512
VMEM_LIMIT = 56 * 1024 * 1024


def dot(a, b):
    return lax.dot_general(a, b, (((1,), (0,)), ((), ())), preferred_element_type=F32)


def dot_t(a, b):
    return lax.dot_general(a, b, (((1,), (1,)), ((), ())), preferred_element_type=F32)


def t_dot(a, b):
    return lax.dot_general(a, b, (((0,), (0,)), ((), ())), preferred_element_type=F32)


def copy_to(src, dst, send_sem, recv_sem, device):
    return pltpu.make_async_remote_copy(
        src_ref=src,
        dst_ref=dst,
        send_sem=send_sem,
        recv_sem=recv_sem,
        device_id=device,
        device_id_type=MESH,
    )


class Place:
    def __init__(self):
        self.section = lax.axis_index("section")
        self.expert = lax.axis_index("expert")
        self.group = lax.axis_index("dp")
        self.half = self.section % 2
        self.pair = self.section // 2
        self.partner = self.section + 1 - 2 * self.half


def greet_experts(here, barrier):
    def one(k, carry):
        pl.semaphore_signal(
            barrier,
            inc=1,
            device_id={"expert": (here.expert + k) % EXPERTS},
            device_id_type=MESH,
        )
        return carry

    lax.fori_loop(1, EXPERTS, one, 0)


def greet(barrier, device):
    pl.semaphore_signal(barrier, inc=1, device_id=device, device_id_type=MESH)


class Exchange:
    def __init__(self, here, src, dst, sems, sign):
        self.here, self.src, self.dst, self.sems, self.sign = here, src, dst, sems, sign

    def copy(self, k, count=1):
        which = pl.ds(k, count)
        peer = (self.here.expert + self.sign * k + EXPERTS) % EXPERTS
        return copy_to(
            self.src.at[which], self.dst.at[which], self.sems.at[0], self.sems.at[1], {"expert": peer}
        )

    def start(self, rows):
        messages = rows.astype(BF16).reshape(EXPERTS, MSG, PART)
        self.src[...] = messages
        self.dst[0:1] = messages[0:1]

        def one(k, carry):
            self.copy(k).start()
            return carry

        lax.fori_loop(1, EXPERTS, one, 0)

    def take(self):
        self.copy(1, EXPERTS - 1).wait_recv()
        return self.dst[...].reshape(SLOTS, PART)

    def wait_send(self):
        self.copy(1, EXPERTS - 1).wait_send()


class GroupSum:
    def __init__(self, here, parts, landed, sems):
        self.here, self.parts, self.landed, self.sems = here, parts, landed, sems

    def part(self, away, half):
        quarter = (self.here.group + away) % GROUPS
        rows = pl.ds(pl.multiple_of(quarter * QUART, QUART), QUART)
        return self.parts.at[rows, pl.ds(half * HALF, HALF)]

    def copy(self, slot):
        away, half, to = ((2, 0, 1), (2, 1, 3), (1, 1, 1), (3, 0, 3), (1, 0, 1), (3, 1, 3))[slot]
        return copy_to(
            self.part(away, half), self.landed.at[slot], self.sems.at[0, slot], self.sems.at[1, slot],
            {"dp": (self.here.group + to) % GROUPS},
        )

    def start(self, near, far):
        self.parts[:, 0:HALF] = near.astype(BF16)
        self.parts[:, HALF:] = far.astype(BF16)
        for slot in range(4):
            self.copy(slot).start()

    def pass_on(self):
        for slot, away in ((0, 1), (1, 3)):
            self.copy(slot).wait_recv()
            part = self.part(away, slot)
            part[...] = (part[...].astype(F32) + self.landed[slot].astype(F32)).astype(BF16)
            self.copy(slot + 4).start()

    def total(self):
        for slot in range(2, 6):
            self.copy(slot).wait_recv()

        def half(i, one, other):
            return self.part(0, i)[...].astype(F32) + self.landed[one].astype(F32) + self.landed[other].astype(F32)

        return jnp.concatenate([half(0, 3, 4), half(1, 2, 5)], axis=1)

    def wait_send(self):
        for slot in range(6):
            self.copy(slot).wait_send()


class GroupGather:
    def __init__(self, here, whole, sems):
        self.here, self.whole, self.sems = here, whole, sems

    def rows(self, back):
        quarter = (self.here.group + GROUPS - back) % GROUPS
        return pl.ds(pl.multiple_of(quarter * QUART, QUART), QUART)

    def copy(self, to, back, half, slot):
        where = self.whole.at[self.rows(back), pl.ds(half * HALF, HALF)]
        return copy_to(
            where, where, self.sems.at[0, slot], self.sems.at[1, slot],
            {"dp": (self.here.group + to) % GROUPS},
        )

    def start(self, value):
        self.whole[self.rows(0)] = value
        for slot, (to, half) in enumerate(((1, 0), (3, 1), (1, 1), (3, 0))):
            self.copy(to, 0, half, slot).start()

    def start_near(self, value):
        self.whole[self.rows(0), 0:HALF] = value
        self.copy(1, 0, 0, 0).start()
        self.copy(3, 0, 0, 3).start()

    def start_far(self):
        self.copy(3, 0, 1, 1).start()
        self.copy(1, 0, 1, 2).start()

    def pass_on(self):
        self.copy(1, 1, 0, 0).wait_recv()
        self.copy(1, 1, 0, 4).start()
        self.copy(3, 3, 1, 1).wait_recv()
        self.copy(3, 3, 1, 5).start()

    def wait_recv(self):
        self.copy(1, 1, 1, 2).wait_recv()
        self.copy(3, 3, 0, 3).wait_recv()
        self.copy(1, 2, 0, 4).wait_recv()
        self.copy(3, 2, 1, 5).wait_recv()

    def wait_send(self):
        for slot, (to, half) in enumerate(((1, 0), (3, 1), (1, 1), (3, 0))):
            self.copy(to, 0, half, slot).wait_send()
        self.copy(1, 1, 0, 4).wait_send()
        self.copy(3, 3, 1, 5).wait_send()


class SmallSum:
    def __init__(self, here, own, landed, sems):
        self.here, self.own, self.landed, self.sems = here, own, landed, sems

    def copy(self, j):
        return copy_to(
            self.own,
            self.landed.at[j - 1],
            self.sems.at[0, j - 1],
            self.sems.at[1, j - 1],
            {"dp": (self.here.group + j) % GROUPS},
        )

    def start(self):
        for j in (2, 1, 3):
            self.copy(j).start()

    def start_column(self, column):
        self.own[...] = jnp.broadcast_to(column, (TOKENS, TOKENS)).T[0:8]
        self.start()

    def total(self):
        for j in (1, 3, 2):
            self.copy(j).wait_recv()
        return self.own[...] + self.landed[0] + self.landed[1] + self.landed[2]

    def total_column(self):
        return jnp.broadcast_to(self.total()[0:1], (TOKENS, TOKENS)).T[:, 0:1]

    def wait_send(self):
        for j in (1, 2, 3):
            self.copy(j).wait_send()


class HandOn:
    def __init__(self, here, leaving, handed, sems):
        self.here, self.leaving, self.handed, self.sems = here, leaving, handed, sems

    def copy(self, to, owner):
        return copy_to(
            self.leaving, self.handed.at[owner], self.sems.at[0, to], self.sems.at[1, owner],
            {"section": 2 * (1 - self.here.pair) + to},
        )

    def start(self, value):
        self.leaving[...] = value.astype(BF16)
        for to in range(2):
            self.copy(to, self.here.half).start()

    def take(self):
        for owner in range(2):
            self.copy(0, owner).wait_recv()
        return (self.handed[0].astype(F32) + self.handed[1].astype(F32)).astype(BF16)

    def again(self):
        return (self.handed[0].astype(F32) + self.handed[1].astype(F32)).astype(BF16)

    def wait_send(self):
        for to in range(2):
            self.copy(to, self.here.half).wait_send()


class Cut:
    def __init__(self, here, source, middle, target, sems, flip):
        self.here, self.source, self.middle, self.target = here, source, middle, target
        self.sems, self.flip = sems, flip

    def rows(self, m, section):
        pair = section // 2
        return self.source.at[1 - pair if self.flip else pair, m]

    def across(self, m, j, owner):
        to = (self.here.section + j) % 4
        return copy_to(
            self.rows(m, to), self.middle.at[m, owner],
            self.sems.at[0, 0, m, j - 1], self.sems.at[0, 1, m, j - 1], {"section": to},
        )

    def within(self, m, j, owner):
        to = (self.here.group + j) % GROUPS
        return copy_to(
            self.middle.at[m, to], self.target.at[m, owner],
            self.sems.at[1, 0, m, j - 1], self.sems.at[1, 1, m, j - 1], {"dp": to},
        )

    def start(self, m):
        for j in (2, 1, 3):
            self.across(m, j, self.here.section).start()
        self.middle[m, pl.ds(self.here.section, 1)] = self.rows(m, self.here.section)[...][None]

    def pass_on(self, m):
        for j in (1, 3, 2):
            self.across(m, j, (self.here.section + 4 - j) % 4).wait_recv()
        for j in (2, 1, 3):
            self.within(m, j, self.here.group).start()
        own = pl.ds(self.here.group, 1)
        self.target[m, own] = self.middle[m, own]

    def take(self, m):
        for j in (1, 3, 2):
            self.within(m, j, (self.here.group + GROUPS - j) % GROUPS).wait_recv()

    def value(self, m):
        return self.target[m].reshape(TOKENS, PART)

    def wait_send(self):
        for m in range(BATCHES):
            for j in (1, 2, 3):
                self.across(m, j, self.here.section).wait_send()
                self.within(m, j, self.here.group).wait_send()


class Routes:
    def __init__(self, rows, columns):
        self.rows, self.columns = rows, columns

    def by_slot(self, u, m):
        slots = lax.broadcasted_iota(jnp.int32, (SLOTS, TOKENS), 0).astype(F32)
        at = m * 8 + u * 4
        return [(slots == self.rows[at + 2 * k : at + 2 * k + 1], self.rows[at + 2 * k + 1 : at + 2 * k + 2]) for k in range(2)]

    def by_token(self, u, m):
        slots = lax.broadcasted_iota(jnp.int32, (TOKENS, SLOTS), 1).astype(F32)
        at = m * 8 + u * 4
        return [(slots == self.columns[:, at + 2 * k : at + 2 * k + 1], self.columns[:, at + 2 * k + 1 : at + 2 * k + 2]) for k in range(2)]


def marks(picks):
    (first, _), (second, _) = picks
    return jnp.where(first | second, 1.0, 0.0).astype(BF16)


def weighted(picks):
    (first, share), (second, other) = picks
    return jnp.where(first, share, 0.0) + jnp.where(second, other, 0.0)


def exact_dot(weights, values):
    high = weights.astype(BF16)
    low = (weights - high.astype(F32)).astype(BF16)
    return dot(high, values) + dot(low, values)


def norm_scale(total):
    return lax.rsqrt(total * (1.0 / (GROUPS * PART)) + EPSILON)


def silu(pre):
    return pre * jax.nn.sigmoid(pre)


def pre_gradient(act_grad, pre):
    gate = jax.nn.sigmoid(pre)
    return (act_grad * gate * (1.0 + pre * (1.0 - gate))).astype(BF16)


def row_sum(values):
    return jnp.sum(values, axis=1, keepdims=True)


def update(
    stream, cotangent, up, down, norm_gain, routes_own,
    grad_up, grad_down,
    middle_in, middle_cotan, layer_in, cotan, up_other, down_other, routes_landed, routes_rows, routes_columns,
    sent, came, rows1, rows1_other, rows2, grads1, grads2, parts, landed, gathered, pre1, pre2,
    small_own, small_landed, scales, leaving, handed,
    sum_up, sum_down, give_up, give_down, got_up, got_down, far_quarter,
    cut_sems, pair_sems, far_sems, route_sems, small_sems, peer_sems, sum_sems, gather_sems, hand_sems,
):
    here = Place()
    both = range(BATCHES)
    barrier = pltpu.get_barrier_semaphore()
    greet_experts(here, barrier)

    def greet_other(i, carry):
        at = (here.section * GROUPS + here.group + i) % 16
        greet(barrier, {"section": at // GROUPS, "dp": at % GROUPS})
        return carry

    lax.fori_loop(1, 16, greet_other, 0)
    pl.semaphore_wait(barrier, EXPERTS - 1 + 15)

    def exchanges(i, sign):
        return [Exchange(here, sent.at[i, m], came.at[i, m], peer_sems.at[i, m], sign) for m in both]

    go1, back1, go_grads, go2, back2, go3 = (
        exchanges(i, sign) for i, sign in enumerate((1, -1, 1, 1, -1, 1))
    )
    sum1, sum2, sum_grads2, sum_grads1 = (
        [GroupSum(here, parts.at[i, m], landed.at[i, m], sum_sems.at[i, m]) for m in both] for i in range(4)
    )
    act1, act2, pre_grad2, pre_grad1 = ([gathered.at[i, m] for m in both] for i in range(4))
    all_act1, all_act2, all_pre_grad2, all_pre_grad1 = (
        [GroupGather(here, gathered.at[i, m], gather_sems.at[i, m]) for m in both] for i in range(4)
    )
    norm1, norm2, mix = (
        [SmallSum(here, small_own.at[i, m], small_landed.at[i, m], small_sems.at[i, m]) for m in both]
        for i in range(3)
    )
    hand1, hand2 = (
        [HandOn(here, leaving.at[i, m], handed.at[i, m], hand_sems.at[i, m]) for m in both] for i in range(2)
    )
    cut_in = Cut(here, stream, middle_in, layer_in, cut_sems.at[0], False)
    cut_cotan = Cut(here, cotangent, middle_cotan, cotan, cut_sems.at[1], True)
    route_sum = SmallSum(here, routes_own, routes_landed, route_sems)
    routes = Routes(routes_rows, routes_columns)
    to_partner = {"section": here.partner}

    def pair_copy(i, source, target):
        return copy_to(source, target, pair_sems.at[0, i], pair_sems.at[1, i], to_partner)

    up_copy, down_copy = pair_copy(0, up, up_other), pair_copy(1, down, down_other)
    give_down_copy, give_up_copy = pair_copy(2, give_down, got_down), pair_copy(3, give_up, got_up)
    rows_copy = pair_copy(4, rows1, rows1_other)
    own_quarter = pl.ds(pl.multiple_of(here.group * QUART, QUART), QUART)
    far_copies = [
        copy_to(
            far_quarter.at[m], gathered.at[3, m, own_quarter, pl.ds(HALF, HALF)],
            far_sems.at[0, m], far_sems.at[1, m], to_partner,
        )
        for m in both
    ]
    gain = norm_gain[pl.ds(here.pair, 1), pl.ds(pl.multiple_of(here.group * PART, PART), PART)]
    first_half = (1 - here.half).astype(F32)

    def up_parts(rows, target):
        target.start(dot(rows[...], up[...]), dot(rows[...], up_other[...]))

    def down_parts(rows, target):
        target.start(dot_t(rows[...], down[...]), dot_t(rows[...], down_other[...]))

    route_sum.start()
    for m in both:
        cut_in.start(m)
    for m in both:
        cut_cotan.start(m)
    for m in both:
        cut_in.pass_on(m)
    up_copy.start()
    for m in both:
        cut_in.take(m)
        values = cut_in.value(m).astype(F32)
        norm1[m].start_column(row_sum(values * values))
    total = route_sum.total()
    routes_rows[...] = total
    routes_columns[...] = jnp.concatenate([total] * (TOKENS // total.shape[0]), axis=0).T
    spreads = [marks(routes.by_slot(0, m)) for m in both]
    for m in both:
        scale = norm_scale(norm1[m].total_column())
        normed = (cut_in.value(m).astype(F32) * scale * gain).astype(BF16)
        go1[m].start(dot(spreads[m], normed))
    for m in both:
        cut_cotan.pass_on(m)
    up_copy.wait_recv()
    down_copy.start()

    def take_rows1(m):
        rows1[m] = go1[m].take()
        up_parts(rows1.at[m], sum1[m])

    def start_grads2(m):
        cut_cotan.take(m)
        go_grads[m].start(exact_dot(weighted(routes.by_slot(1, m)), cut_cotan.value(m)))

    def take_grads2(m):
        grads2[m] = go_grads[m].take()
        down_parts(grads2.at[m], sum_grads2[m])

    def activate1(m):
        pre1[m] = sum1[m].total()
        all_act1[m].start(silu(pre1[m]).astype(BF16))

    def expert_out1(m):
        all_act1[m].wait_recv()
        act = act1[m]
        back1[m].start(dot(act[:, 0:HALF], down[...]) + dot(act[:, HALF:], down_other[...]))

    def leave1(m):
        weights = weighted(routes.by_token(0, m))
        direct = cut_in.value(m).astype(F32) * first_half
        hand1[m].start(direct + exact_dot(weights, back1[m].take()))

    take_rows1(0)
    sum1[0].pass_on()
    start_grads2(0)
    take_rows1(1)
    activate1(0)
    sum1[1].pass_on()
    all_act1[0].pass_on()
    down_copy.wait_recv()
    expert_out1(0)
    activate1(1)
    all_act1[1].pass_on()
    expert_out1(1)
    take_grads2(0)
    leave1(0)
    sum_grads2[0].pass_on()
    leave1(1)
    start_grads2(1)

    def arrive2(m):
        values = hand1[m].take().astype(F32)
        norm2[m].start_column(row_sum(values * values))
        spread = marks(routes.by_slot(1, m))
        scales[m] = norm_scale(norm2[m].total_column())
        normed = (hand1[m].again().astype(F32) * scales[m] * gain).astype(BF16)
        go2[m].start(dot(spread, normed))

    def take_rows2(m):
        rows2[m] = go2[m].take()
        up_parts(rows2.at[m], sum2[m])

    def activate2(m):
        pre2[m] = sum2[m].total()
        all_pre_grad2[m].start(pre_gradient(sum_grads2[m].total(), pre2[m]))

    def row_grads2(m):
        all_pre_grad2[m].wait_recv()
        grad = pre_grad2[m]
        back2[m].start(dot_t(grad[:, 0:HALF], up[...]) + dot_t(grad[:, HALF:], up_other[...]))

    arrive2(0)
    arrive2(1)
    take_grads2(1)
    rows_copy.start()
    take_rows2(0)
    sum_grads2[1].pass_on()
    sum2[0].pass_on()
    take_rows2(1)
    activate2(0)
    sum2[1].pass_on()
    all_pre_grad2[0].pass_on()
    row_grads2(0)
    activate2(1)
    all_pre_grad2[1].pass_on()
    row_grads2(1)
    def collect2(m):
        collect = marks(routes.by_token(1, m))
        scaled = dot(collect, back2[m].take()) * gain
        mix[m].start_column(row_sum(hand1[m].again().astype(F32) * scaled))
        return scaled

    def leave2(m, scaled):
        direct = cut_cotan.value(m).astype(F32) * first_half + scales[m] * scaled
        mean = mix[m].total_column() * (1.0 / (GROUPS * PART))
        scale = scales[m]
        hand2[m].start(direct - hand1[m].again().astype(F32) * (scale * scale * scale * mean))

    scaled = collect2(0)
    for m in both:
        all_act2[m].start(silu(pre2[m]).astype(BF16))
    leave2(0, scaled)

    @pl.loop(0, PART // 128)
    def _(i):
        at = pl.ds(pl.multiple_of(i * 128, 128), 128)
        value = t_dot(rows2[0, :, at], pre_grad2[0][...]) + t_dot(rows2[1, :, at], pre_grad2[1][...])
        sum_up[at] = value[:, 0:HALF]
        give_up[at] = value[:, HALF:].astype(BF16)

    scaled = collect2(1)
    for m in both:
        all_act2[m].pass_on()
    leave2(1, scaled)
    for m in both:
        all_act2[m].wait_recv()

    def arrive1(m):
        weights = weighted(routes.by_slot(0, m))
        go3[m].start(exact_dot(weights, hand2[m].take()))

    arrive1(0)

    @pl.loop(0, 2 * HALF // 128)
    def _(i):
        at = pl.ds(pl.multiple_of(i * 128, 128), 128)
        sum_down[at] = t_dot(act2[0][:, at], grads2[0]) + t_dot(act2[1][:, at], grads2[1])

    arrive1(1)
    give_up_copy.start()
    def take_grads1(m):
        grads1[m] = go3[m].take()
        down_parts(grads1.at[m], sum_grads1[m])

    def pre_grads1(m):
        quarter = pre_gradient(sum_grads1[m].total(), pre1[m])
        far_quarter[m] = quarter[:, HALF:]
        far_copies[m].start()
        all_pre_grad1[m].start_near(quarter[:, 0:HALF])

    def far_pre_grads1(m):
        far_copies[m].wait_recv()
        all_pre_grad1[m].start_far()

    take_grads1(0)
    sum_grads1[0].pass_on()
    take_grads1(1)
    pre_grads1(0)
    sum_grads1[1].pass_on()
    far_pre_grads1(0)

    @pl.loop(0, HALF // 128)
    def _(i):
        at = pl.ds(pl.multiple_of(i * 128, 128), 128)
        far = pl.ds(pl.multiple_of(HALF + i * 128, 128), 128)
        value = sum_down[far] + t_dot(act1[0][:, far], grads1[0]) + t_dot(act1[1][:, far], grads1[1])
        give_down[at] = value.astype(BF16)

    pre_grads1(1)
    give_down_copy.start()
    all_pre_grad1[0].pass_on()
    far_pre_grads1(1)
    all_pre_grad1[1].pass_on()

    @pl.loop(0, HALF // 128)
    def _(i):
        at = pl.ds(pl.multiple_of(i * 128, 128), 128)
        sum_down[at] += t_dot(act1[0][:, at], grads1[0]) + t_dot(act1[1][:, at], grads1[1])

    give_up_copy.wait_recv()
    sum_up[...] += got_up[...].astype(F32)
    rows_copy.wait_recv()
    def rows_grads1(m, at):
        own = t_dot(rows1[m, :, at], pre_grad1[m][:, 0:HALF])
        return own + t_dot(rows1_other[m, :, at], pre_grad1[m][:, HALF:])

    all_pre_grad1[0].wait_recv()

    @pl.loop(0, PART // 128)
    def _(i):
        at = pl.ds(pl.multiple_of(i * 128, 128), 128)
        sum_up[at] += rows_grads1(0, at)

    all_pre_grad1[1].wait_recv()

    @pl.loop(0, PART // 128)
    def _(i):
        at = pl.ds(pl.multiple_of(i * 128, 128), 128)
        grad_up[at] = (sum_up[at] + rows_grads1(1, at)).astype(BF16)

    give_down_copy.wait_recv()
    grad_down[...] = (sum_down[0:HALF] + got_down[...].astype(F32)).astype(BF16)

    for sender in (cut_in, cut_cotan, route_sum, up_copy, down_copy, give_down_copy, give_up_copy, rows_copy, *far_copies):
        sender.wait_send()
    for senders in (go1, back1, go_grads, go2, back2, go3, sum1, sum2, sum_grads2, sum_grads1, all_act1,
                    all_act2, all_pre_grad2, all_pre_grad1, norm1, norm2, mix, hand1, hand2):
        for m in both:
            senders[m].wait_send()


def routing(route_ids, route_gates, pair, half):
    ids = lax.dynamic_index_in_dim(route_ids, pair, 0, keepdims=False)
    gates = lax.dynamic_index_in_dim(route_gates, pair, 0, keepdims=False)
    shares = gates / jnp.sum(gates, axis=-1, keepdims=True)
    ids, shares = (jnp.where(pair == 0, value, value[::-1]) for value in (ids, shares))
    uses, batches, tokens, top = ids.shape
    flat = ids.reshape(uses, batches, tokens * top)
    before = jnp.tri(tokens * top, k=-1, dtype=jnp.bool_)
    position = jnp.sum((flat[..., :, None] == flat[..., None, :]) & before, axis=-1)
    away = (flat - lax.axis_index("expert") + EXPERTS) % EXPERTS
    group = lax.axis_index("dp")
    slot = away * MSG + group * 2 + position % 2
    slot = jnp.where(position // 2 == half, slot, -1).astype(F32).reshape(ids.shape)
    values = jnp.stack([slot, shares], axis=-1).transpose(1, 0, 3, 4, 2).reshape(batches * uses * top * 2, tokens)
    lanes = jnp.arange(TOKENS, dtype=jnp.int32)[None, :] // BLOCK
    return jnp.where(lanes == group, jnp.tile(values, (1, GROUPS)), 0.0)


def local(stream_in, cotangent, route_ids, route_gates, norm_gain, up_weight, down_weight):
    section = lax.axis_index("section")
    routes = routing(route_ids, route_gates, section // 2, section % 2)
    dma, vmem = pltpu.SemaphoreType.DMA, pltpu.VMEM
    whole = pl.BlockSpec(memory_space=pltpu.VMEM)
    messages = vmem((6, BATCHES, EXPERTS, MSG, PART), BF16)
    features = vmem((BATCHES, SLOTS, PART), BF16)
    hidden = vmem((4, BATCHES, SLOTS, 2 * HALF), BF16)
    quarters = vmem((BATCHES, QUART, 2 * HALF), F32)
    cut = vmem((BATCHES, GROUPS, BLOCK, PART), BF16)
    up_half, down_half = vmem((PART, HALF), BF16), vmem((HALF, PART), BF16)
    scratch = [
        cut, cut, cut, cut, up_half, down_half,
        vmem((3, 16, TOKENS), F32), vmem((16, TOKENS), F32), vmem((TOKENS, TOKENS), F32),
        messages, messages, features, features, features, features, features,
        hidden, vmem((4, BATCHES, 6, QUART, HALF), BF16), hidden, quarters, quarters,
        vmem((3, BATCHES, 8, TOKENS), F32), vmem((3, BATCHES, 3, 8, TOKENS), F32), vmem((BATCHES, TOKENS, 1), F32),
        vmem((2, BATCHES, TOKENS, PART), BF16), vmem((2, BATCHES, 2, TOKENS, PART), BF16),
        vmem((PART, HALF), F32), vmem((2 * HALF, PART), F32),
        up_half, down_half, up_half, down_half, vmem((BATCHES, QUART, HALF), BF16),
        dma((2, 2, 2, BATCHES, 3)), dma((2, 5)), dma((2, BATCHES)), dma((2, 3)), dma((3, BATCHES, 2, 3)), dma((6, BATCHES, 2)),
        dma((4, BATCHES, 2, 6)), dma((4, BATCHES, 2, 6)), dma((2, BATCHES, 2, 2)),
    ]
    grad_up, grad_down = pl.pallas_call(
        update,
        out_shape=[jax.ShapeDtypeStruct((PART, HALF), BF16), jax.ShapeDtypeStruct((HALF, PART), BF16)],
        in_specs=[whole] * 6,
        out_specs=[whole] * 2,
        scratch_shapes=scratch,
        compiler_params=pltpu.CompilerParams(
            collective_id=0, has_side_effects=True, vmem_limit_bytes=VMEM_LIMIT
        ),
    )(stream_in, cotangent, up_weight[0, 0], down_weight[0, 0], norm_gain, routes)
    return grad_up[None, None], grad_down[None, None]


def solution(mesh):
    placed = (
        P(None, None, ("expert", "dp"), "section"),
        P(None, None, ("expert", "dp"), "section"),
        P(None, None, None, ("expert", "dp"), None),
        P(None, None, None, ("expert", "dp"), None),
        P(),
        P("section", "expert", "dp", None),
        P("section", "expert", None, "dp"),
    )
    return jax.shard_map(
        local,
        mesh=mesh,
        in_specs=placed,
        out_specs=(P("section", "expert", "dp", None), P("section", "expert", None, "dp")),
        check_vma=False,
    )
```
